128 devices in a mesh: row: 8 (over y, core), col: 16 (over z, x).
Axes of the slice: x: 4, y: 4, z: 4, core: 2. Of those that a mesh axis runs over, the one named last changes fastest.
Arguments:
- integrals: bfloat16 [8, 16, 32, 512, 512], P('row', 'col'), may hold values from -0.046875 to 0.046875
- tile_count: int32 [8, 16], P('row', 'col'), may hold values from 1 to 32, as said below
- tile_list: int32 [8, 16, 32], P('row', 'col'), may hold values from 0 to 31, as said below
- amplitudes: bfloat16 [64, 512, 1024], P('col', 'row'), may hold values from -6 to 6
- pair_energy: float32 [32768], P(('row', 'col')), may hold values from 1 to 4
- occ_energy: float32 [32], replicated, may hold values from -1.5 to -0.25
- partner: int32 [32768], P(('row', 'col')), may hold values from 0 to 32767, as said below
Outputs:
- amp_update: float32 [32768, 1024], P(('row', 'col'))
The draws below stay inside these ranges and needn't reach their ends.
Inputs may be any that keep to these rules, and one draw needn't show every extreme that they name: `tile_count`: some grid cell holds exactly 32 live tiles. `tile_list`: each grid cell's list is a permutation of 0 to 31; only its first tile_count entries name live tiles. partner is an involution. Numbering the rows in consecutive blocks of 256, the rows of one block have their partners among the 16 blocks of the same aligned group of 4096 rows, exactly 16 of them in each of these blocks.
All inputs are finite; a program needn't handle non-finite values.
Results may differ from the reference program's by a relative error of at most 0.0003.
Values may be sent and summed in bfloat16 or wider, within the bound.
No kernel may reach another device: no remote copies, remote signals or barrier semaphores. Data moves between devices by JAX's collectives and lax.ppermute only.
A program may use at most 128 MiB of HBM per device.

```python
import math
import jax
import jax.numpy as jnp
from jax import lax

TILE = 512
NO = 32
BC = 4
OCC = 1024
NBLK = 64
BR = 8
CAP = 32
NPAIRS = 32768
ROWS = 256
PEER = 16
N_ROW = 8
N_COL = 16


def shuffle_cap(subkey):
    return jax.random.permutation(subkey, CAP).astype(jnp.int32)


def shuffle_rows(subkey):
    return jax.random.permutation(subkey, ROWS).astype(jnp.int32)


def draw_tile_count(key, part):
    counts = jax.random.randint(key, (N_ROW * N_COL,), 1, CAP + 1).astype(jnp.int32)
    chosen = jax.random.randint(jax.random.fold_in(key, 7), (), 0, N_ROW * N_COL)
    counts = jnp.where(jnp.arange(N_ROW * N_COL) == chosen, CAP, counts)
    return counts.reshape(N_ROW, N_COL).astype(jnp.int32)


def draw_tile_list(key, part):
    subkeys = jax.random.split(jax.random.fold_in(key, 11), N_ROW * N_COL)
    orders = jax.vmap(shuffle_cap)(subkeys)
    return orders.reshape(N_ROW, N_COL, CAP).astype(jnp.int32)


def draw_partner(key, part):
    subkeys = jax.random.split(jax.random.fold_in(key, 13), N_ROW * N_COL)
    orders = jax.vmap(shuffle_rows)(subkeys).reshape(N_ROW, N_COL, ROWS)
    inverse = jnp.argsort(orders, axis=2).astype(jnp.int32)
    target = inverse // PEER
    within = inverse % PEER
    grid_row = jnp.arange(N_ROW, dtype=jnp.int32)[:, None, None]
    grid_col = jnp.arange(N_COL, dtype=jnp.int32)[None, :, None]
    local_row = orders[grid_row, target, grid_col * PEER + within]
    result = (grid_row * N_COL + target) * ROWS + local_row
    return result.reshape(N_ROW * N_COL * ROWS).astype(jnp.int32)


def block_levels(stream_key, dims, cuts, least, largest):
    gain, own = 1.0, jax.random.fold_in(stream_key, 6)
    for axis_at, blocks in cuts:
        draws = jnp.exp(jax.random.uniform(jax.random.fold_in(own, axis_at), (blocks,), jnp.float32, least / len(cuts), largest / len(cuts)))
        gain = gain * jnp.repeat(draws, dims[axis_at] // blocks).reshape([-1 if axis == axis_at else 1 for axis in range(len(dims))])
    return gain


def noise(rng, dims, spread, most, cuts=(), held_as=jnp.bfloat16):
    drawn = spread * jax.random.normal(rng, dims, jnp.float32)
    if cuts:
        drawn = drawn * block_levels(rng, dims, cuts, -0.22, 0.18)
    return jnp.clip(drawn, -most, most).astype(held_as)


def setup_inputs(seed: int = 0) -> dict:
    key_list = jax.random.split(jax.random.key(seed), 8)
    return {
        "integrals": noise(key_list[0], (N_ROW, N_COL, CAP, TILE, TILE), (NBLK * TILE // 2) ** -0.5, 0.046875, ((0, 8), (1, 16))),
        "tile_count": draw_tile_count(jax.random.fold_in(key_list[7], 71), 0),
        "tile_list": draw_tile_list(jax.random.fold_in(key_list[7], 71), 0),
        "amplitudes": noise(key_list[3], (NBLK, TILE, OCC), 1.0, 6.0, ((0, 16), (1, 8))),
        "pair_energy": jnp.clip(jnp.exp(math.log(4.0) - 1.3862944 * jax.random.uniform(key_list[4], (NPAIRS,), jnp.float32) ** block_levels(key_list[4], (NPAIRS,), ((0, 128),), -0.2, 0.2)), 1.0, 4.0),
        "occ_energy": jnp.clip(jax.random.uniform(key_list[5], (NO,), jnp.float32, -1.5, -0.25), -1.5, -0.25),
        "partner": draw_partner(jax.random.fold_in(key_list[7], 71), 0),
    }


def reference(integrals, tile_count, tile_list, amplitudes, pair_energy, occ_energy, partner):
    residual = jnp.zeros((NBLK, TILE, OCC), jnp.float32)

    def per_device(device, running):
        grid_row = (device // N_COL).astype(jnp.int32)
        grid_col = (device % N_COL).astype(jnp.int32)
        count_here = tile_count[grid_row, grid_col]

        def per_slot(slot, inner):
            position = tile_list[grid_row, grid_col, slot]
            block_row = grid_row * BR + position // BC
            block_col = grid_col * BC + position % BC
            product = jnp.dot(integrals[grid_row, grid_col, slot], amplitudes[block_col], preferred_element_type=jnp.float32)
            current = lax.dynamic_index_in_dim(inner, block_row, 0, keepdims=False)
            return lax.dynamic_update_index_in_dim(inner, current + product, block_row, 0)

        return lax.fori_loop(0, count_here, per_slot, running)

    residual = lax.fori_loop(0, N_ROW * N_COL, per_device, residual)
    flat_rows = residual.reshape(NPAIRS, OCC)
    mirrored = jnp.take(flat_rows, partner, axis=0).reshape(NPAIRS, NO, NO)
    mirrored = jnp.swapaxes(mirrored, 1, 2).reshape(NPAIRS, OCC)
    denominator = pair_energy[:, None] - (occ_energy[:, None] + occ_energy[None, :]).reshape(1, OCC)
    return (flat_rows + mirrored) / denominator
```

```python
import functools

import numpy as np
import jax
import jax.numpy as jnp
from jax import lax
from jax.experimental import pallas as pl
from jax.experimental.pallas import tpu as pltpu
from jax.sharding import PartitionSpec as P

F32, S32, S16, BF16 = jnp.float32, jnp.int32, jnp.int16, jnp.bfloat16
NO = 32
OCC = NO * NO
HALF = OCC // 2
CHUNKS = 2
CW = OCC // CHUNKS
LANES = 128
SIDE = 4
PAD = 16
LOG_GRID = 200.0
FULL = 32760.0
TINY = 1e-37
VMEM = 56 * 1024 * 1024


def pair_orders():
    first, mates = [], []
    for gap in range(1, NO // 2):
        for i in range(NO):
            j = (i + gap) % NO
            first.append(i * NO + j)
            mates.append(j * NO + i)
    first += [i * NO + i for i in range(NO)]
    mates += [i * NO + i + NO // 2 for i in range(NO // 2)]
    mates += [(i + NO // 2) * NO + i for i in range(NO // 2)]
    return np.array(first, np.int32), np.array(mates, np.int32)


def column_scale(level):
    return jnp.ceil(jnp.log(jnp.maximum(level, TINY)) * (LOG_GRID / float(np.log(2.0))))


def encode(values, scale):
    return jnp.round(values * (jnp.exp2(scale * (-1.0 / LOG_GRID)) * FULL)).astype(S32).astype(S16)


def decode(coded, scale):
    return coded.astype(S32).astype(F32) * (jnp.exp2(scale * (1.0 / LOG_GRID)) * (1.0 / FULL))


def pack(out_ref, values, far):
    rows = values.shape[0]
    scale = column_scale(jnp.max(jnp.abs(values), axis=0, keepdims=True))
    out_ref[pl.ds(0, rows), :] = encode(values, scale)
    heads = jnp.broadcast_to(scale, (PAD, LANES))
    if far is None:
        out_ref[pl.ds(rows, PAD), :] = heads.astype(S32).astype(S16)
        return
    far_scale = column_scale(jnp.max(jnp.abs(far), axis=0, keepdims=True))
    out_ref[pl.ds(rows, PAD), :] = encode(far, far_scale)
    which = lax.broadcasted_iota(S32, (PAD, LANES), 0)
    heads = jnp.where(which == 0, heads, jnp.broadcast_to(far_scale, (PAD, LANES)))
    out_ref[pl.ds(rows + PAD, PAD), :] = heads.astype(S32).astype(S16)


def unpack_sum(refs, rows, has_far):
    total, far = None, None
    for ref in refs:
        heads = ref[pl.ds(rows + (PAD if has_far else 0), PAD), :].astype(S32).astype(F32)
        part = decode(ref[pl.ds(0, rows), :], heads[0:1])
        total = part if total is None else total + part
        if has_far:
            part = decode(ref[pl.ds(rows, PAD), :], heads[1:2])
            far = part if far is None else far + part
    return total, far


def product_kernel(has_far, rows, order_ref, live_ref, mate_ref, place_ref, v0, v1, v2, v3, t_ref, *rest):
    outs, (prod, moved) = rest[:8], rest[8:]
    step = pl.program_id(0)
    tile = v0.shape[1]
    half = CW // 2
    for part in range(2):
        total = None
        for j, v_ref in enumerate((v0, v1, v2, v3)):
            live = live_ref[step * 4 + j] > 0
            v = jnp.where(live, v_ref[0], jnp.zeros((), BF16))
            t = t_ref[:, j, :, pl.ds(part * half, half)].reshape(tile, half)
            add = jnp.dot(v, t, preferred_element_type=F32)
            total = add if total is None else total + add
        prod[pl.ds(pl.multiple_of(step * tile, tile), tile), pl.ds(part * half, half)] = total

    @pl.when(step == pl.num_programs(0) - 1)
    def _():
        z, x = place_ref[0], place_ref[1]
        for kx in range(SIDE):
            for kz in range(SIDE):
                zt = lax.rem(z + kz, SIDE)
                xt = lax.rem(x + kx, SIDE)
                base = pl.multiple_of((zt * SIDE + xt) * rows, rows)

                def gather(turn, carry):
                    for member in range(16):
                        at = turn * 16 + member
                        mate = mate_ref[base + at]
                        moved[pl.ds(at, 1), :] = prod[pl.ds(mate, 1), pl.ds(half, half)]
                    return carry

                lax.fori_loop(0, rows // 16, gather, 0)
                for side in range(2):
                    mine = prod[pl.ds(base, rows), pl.ds(side * LANES, LANES)]
                    other = moved[:, pl.ds(side * LANES, LANES)]
                    if has_far and side == 1:
                        lane = lax.broadcasted_iota(S32, (rows, LANES), 1)
                        far = prod[pl.ds(base, rows), pl.ds(half + LANES, LANES)]
                        far = (far + pltpu.roll(other, LANES - 16, 1)).T[96:112]
                        other = jnp.where(lane < 96, other, 0.0)
                    if side == 0:
                        near = mine + other
                    else:
                        far_one = far[:, :LANES] if has_far else None
                        far_two = far[:, LANES:] if has_far else None
                        pack(outs[kx].at[zt], near, far_one)
                        pack(outs[4 + kz].at[xt], mine + other, far_two)


def packed_rows(rows, has_far):
    return rows + PAD * (2 if has_far else 1)


def product(integrals, gathered, order, live, mates, place, rows, has_far):
    tiles, tile, _ = integrals.shape
    height = packed_rows(rows, has_far)
    total = SIDE * SIDE * rows
    spec = lambda j: pl.BlockSpec((1, tile, tile), lambda i, order, live, mates, place: (order[i * 4 + j], 0, 0))
    whole = lambda shape: pl.BlockSpec(shape, lambda i, *_: (0,) * len(shape))
    out = (SIDE, height, LANES)
    return pl.pallas_call(
        functools.partial(product_kernel, has_far, rows),
        out_shape=[jax.ShapeDtypeStruct(out, S16)] * 8,
        grid_spec=pltpu.PrefetchScalarGridSpec(
            num_scalar_prefetch=4,
            grid=(tiles // 4,),
            in_specs=[spec(j) for j in range(4)] + [whole(gathered.shape)],
            out_specs=[whole(out)] * 8,
            scratch_shapes=[pltpu.VMEM((total, CW), F32), pltpu.VMEM((rows, CW // 2), F32)],
        ),
        compiler_params=pltpu.CompilerParams(vmem_limit_bytes=VMEM, dimension_semantics=("arbitrary",)),
        cost_estimate=pl.CostEstimate(
            flops=2 * tiles * tile * tile * CW, bytes_accessed=integrals.size * 2, transcendentals=0
        ),
        name="product",
    )(order, live, mates, place, integrals, integrals, integrals, integrals, gathered)


def relay_kernel(has_far, rows, place_ref, *refs):
    ins, outs = refs[:8], refs[8:]
    for side in range(2):
        for k in range(SIDE):
            at = lax.rem(place_ref[side] + k, SIDE)
            total, far = unpack_sum([r.at[at] for r in ins[side * 4 : side * 4 + 4]], rows, has_far)
            pack(outs[side * 4 + k], total, far)


def relay(pieces, place, rows, has_far):
    height = packed_rows(rows, has_far)
    vmem = pl.BlockSpec(memory_space=pltpu.VMEM)
    return pl.pallas_call(
        functools.partial(relay_kernel, has_far, rows),
        out_shape=[jax.ShapeDtypeStruct((height, LANES), S16)] * 8,
        in_specs=[pl.BlockSpec(memory_space=pltpu.SMEM)] + [vmem] * 8,
        out_specs=[vmem] * 8,
        compiler_params=pltpu.CompilerParams(vmem_limit_bytes=VMEM),
        name="relay",
    )(place, *pieces)


def owner_kernel(rows, far_flags, source_ref, *refs):
    count = 8 * len(far_flags)
    ins, own, send, moved = refs[:count], refs[count], refs[count + 1], refs[count + 2]
    for c, has_far in enumerate(far_flags):
        fars = []
        for side in range(2):
            at = c * 8 + side * 4
            total, far = unpack_sum(ins[at : at + 4], rows, has_far)
            own[:, pl.ds((c * 2 + side) * LANES, LANES)] = total
            fars.append(far)
        if has_far:
            far = jnp.concatenate(fars, axis=1)
            far = jnp.concatenate([jnp.zeros((96, rows), F32), far, jnp.zeros((16, rows), F32)], axis=0)
            own[:, pl.ds(HALF, LANES)] = far.T

    def gather(turn, carry):
        for member in range(16):
            at = turn * 16 + member
            moved[pl.ds(at, 1), :] = own[pl.ds(source_ref[at], 1), :]
        return carry

    lax.fori_loop(0, rows // 16, gather, 0)
    scale = column_scale(jnp.max(jnp.abs(moved[...]), axis=1, keepdims=True))
    send[:, pl.ds(0, HALF)] = encode(moved[:, pl.ds(0, HALF)], scale)
    lane = lax.broadcasted_iota(S32, (rows, LANES), 1)
    far = jnp.round(moved[:, pl.ds(HALF, LANES)] * (jnp.exp2(scale * (-1.0 / LOG_GRID)) * FULL))
    far = jnp.where(lane == 0, jnp.broadcast_to(scale, (rows, LANES)), far)
    send[:, pl.ds(HALF, LANES)] = far.astype(S32).astype(S16)


def owner(pieces, source, rows, far_flags):
    vmem = pl.BlockSpec(memory_space=pltpu.VMEM)
    width = HALF + LANES
    return pl.pallas_call(
        functools.partial(owner_kernel, rows, far_flags),
        out_shape=[jax.ShapeDtypeStruct((rows, width), F32), jax.ShapeDtypeStruct((rows, width), S16)],
        in_specs=[pl.BlockSpec(memory_space=pltpu.SMEM)] + [vmem] * len(pieces),
        out_specs=[vmem] * 2,
        scratch_shapes=[pltpu.VMEM((rows, width), F32)],
        compiler_params=pltpu.CompilerParams(vmem_limit_bytes=VMEM),
        name="owner",
    )(source, *pieces)


def close_kernel(rows, index_ref, own, came, energy, pair_sum, spread, out, plain, fetched, joined):
    width = HALF + LANES
    heads = came[:, pl.ds(HALF, LANES)].astype(S32).astype(F32)
    scale = jnp.exp2(heads[:, 0:1] * (1.0 / LOG_GRID)) * (1.0 / FULL)
    plain[...] = came[...].astype(S32).astype(F32) * scale

    def gather(turn, carry):
        for member in range(16):
            at = turn * 16 + member
            fetched[pl.ds(at, 1), :] = plain[pl.ds(index_ref[at], 1), :]
        return carry

    lax.fori_loop(0, rows // 16, gather, 0)
    lane = lax.broadcasted_iota(S32, (rows, LANES), 1)
    edge = HALF - LANES
    joined[:, pl.ds(0, edge)] = own[:, pl.ds(0, edge)]
    joined[:, pl.ds(HALF, edge)] = fetched[:, pl.ds(0, edge)]
    last_own, last_came = own[:, pl.ds(edge, LANES)], fetched[:, pl.ds(edge, LANES)]
    joined[:, pl.ds(edge, LANES)] = last_own + jnp.where(lane < 96, 0.0, last_came)
    far_own, far_came = own[:, pl.ds(HALF, LANES)], pltpu.roll(fetched[:, pl.ds(HALF, LANES)], 16, 1)
    far = jnp.where(lane < 112, far_own, far_came)
    joined[:, pl.ds(HALF + edge, LANES)] = jnp.where(lane < 96, last_came, far)
    rest = joined[...]
    total = None
    for _ in range(3):
        part = rest.astype(BF16)
        rest = rest - part.astype(F32)
        add = jnp.dot(part, spread[...], preferred_element_type=F32)
        total = add if total is None else total + add
    out[...] = total / (energy[...] - pair_sum[...])


def close(own, came, index, energy, pair_sum, spread, rows):
    vmem = pl.BlockSpec(memory_space=pltpu.VMEM)
    width = HALF + LANES
    return pl.pallas_call(
        functools.partial(close_kernel, rows),
        out_shape=jax.ShapeDtypeStruct((rows, OCC), F32),
        in_specs=[pl.BlockSpec(memory_space=pltpu.SMEM)] + [vmem] * 5,
        out_specs=vmem,
        scratch_shapes=[pltpu.VMEM((rows, width), F32)] * 2 + [pltpu.VMEM((rows, OCC), F32)],
        compiler_params=pltpu.CompilerParams(vmem_limit_bytes=VMEM),
        name="close",
    )(index, own, came, energy, pair_sum, spread)


def shifted(dz, dx):
    return [
        (z * SIDE + x, (z + dz) % SIDE * SIDE + (x + dx) % SIDE) for z in range(SIDE) for x in range(SIDE)
    ]


def spread_out(pieces, across_x_first):
    got = list(pieces)
    for k in (2, 1, 3):
        for side in range(2):
            along_x = (side == 0) == across_x_first
            perm = shifted(0, k) if along_x else shifted(k, 0)
            got[side * 4 + k] = lax.ppermute(pieces[side * 4 + k], "col", perm)
    return got


def body(integrals, tile_count, tile_list, amplitudes, pair_energy, occ_energy, partner):
    rows = partner.shape[0]
    col_count = SIDE * SIDE
    first, mates_of = pair_orders()
    pieces = CW // 2
    column_order = np.concatenate(
        [np.concatenate([first[c * pieces :][:pieces], mates_of[c * pieces :][:pieces]]) for c in range(CHUNKS)]
    )
    pair_ids = jnp.arange(OCC, dtype=S32)
    sort = (pair_ids[:, None] == jnp.asarray(column_order)[None, :]).astype(BF16)
    spread = (jnp.asarray(np.concatenate([first, mates_of]))[:, None] == pair_ids[None, :]).astype(BF16)

    blocks, depth, _ = amplitudes.shape
    sorted_amp = jnp.dot(amplitudes.reshape(blocks * depth, OCC), sort, preferred_element_type=F32).astype(BF16)
    gathered = []
    for c in range(CHUNKS):
        part = sorted_amp[:, c * CW : (c + 1) * CW].reshape(blocks, depth, CW)
        gathered.append(lax.all_gather(part, "row", axis=0))

    all_partners = lax.all_to_all(
        jnp.broadcast_to(partner[None, :], (col_count, rows)), "col", split_axis=0, concat_axis=0, tiled=True
    )
    mates = (all_partners % (col_count * rows)).reshape(-1)
    col = lax.axis_index("col")
    place = jnp.stack([col // SIDE, col % SIDE]).astype(S32)
    slots = tile_list[0, 0]
    slot_ids = jnp.arange(slots.shape[0], dtype=S32)
    order = jnp.sum(jnp.where(slots[None, :] == slot_ids[:, None], slot_ids[None, :], 0), axis=1)
    live = (order < tile_count[0, 0]).astype(S32)

    peer = rows // col_count
    target = partner // rows % col_count
    key_local = partner % rows
    row_ids = jnp.arange(rows, dtype=S32)
    same_target = target[:, None] == target[None, :]
    send_rank = jnp.sum(same_target & (key_local[None, :] < key_local[:, None]), axis=1)
    recv_rank = jnp.sum(same_target & (row_ids[None, :] < row_ids[:, None]), axis=1)
    send_slot = target * peer + send_rank
    source = jnp.sum(jnp.where(send_slot[None, :] == row_ids[:, None], row_ids[None, :], 0), axis=1)
    index = target * peer + recv_rank

    tiles = integrals[0, 0]
    far_flags = tuple(c == CHUNKS - 1 for c in range(CHUNKS))
    landed = []
    for c in range(CHUNKS):
        parts = product(tiles, gathered[c], order, live, mates, place, rows, far_flags[c])
        parts = spread_out(parts, True)
        parts = relay(parts, place, rows, far_flags[c])
        landed += spread_out(parts, False)
    own, send = owner(landed, source, rows, far_flags)
    came = lax.all_to_all(send, "col", split_axis=0, concat_axis=0, tiled=True)
    pair_sum = (occ_energy[:, None] + occ_energy[None, :]).reshape(1, OCC)
    return close(own, came, index, pair_energy[:, None], pair_sum, spread, rows)


def solution(mesh):
    return jax.shard_map(
        body,
        mesh=mesh,
        in_specs=(
            P("row", "col", None, None, None),
            P("row", "col"),
            P("row", "col", None),
            P("col", "row", None),
            P(("row", "col")),
            P(),
            P(("row", "col")),
        ),
        out_specs=P(("row", "col"), None),
        check_vma=False,
    )
```

```python
import functools

import numpy as np
import jax
import jax.numpy as jnp
from jax import lax
from jax.experimental import pallas as pl
from jax.experimental.pallas import tpu as pltpu
from jax.sharding import PartitionSpec as P

F32, S32, S16, BF16 = jnp.float32, jnp.int32, jnp.int16, jnp.bfloat16
NO = 32
OCC = NO * NO
HALF = OCC // 2
CHUNKS = 2
CW = OCC // CHUNKS
LANES = 128
SIDE = 4
PAD = 16
LOG_GRID = 200.0
FULL = 32760.0
TINY = 1e-37
VMEM = 28 * 1024 * 1024
SMALL = 16 * 1024 * 1024


def pair_orders():
    first, mates = [], []
    for gap in range(1, NO // 2 + 1):
        for i in range(NO if gap < NO // 2 else NO // 2):
            j = (i + gap) % NO
            first.append(i * NO + j)
            mates.append(j * NO + i)
    first += [i * NO + i for i in range(NO // 2)]
    mates += [i * NO + i for i in range(NO // 2, NO)]
    return np.array(first, np.int32), np.array(mates, np.int32)


def column_scale(level):
    return jnp.ceil(jnp.log(jnp.maximum(level, TINY)) * (LOG_GRID / float(np.log(2.0))))


def encode(values, scale):
    return jnp.round(values * (jnp.exp2(scale * (-1.0 / LOG_GRID)) * FULL)).astype(S32).astype(S16)


def decode(coded, scale):
    return coded.astype(S32).astype(F32) * (jnp.exp2(scale * (1.0 / LOG_GRID)) * (1.0 / FULL))


def pack(out_ref, values, far):
    rows = values.shape[0]
    scale = column_scale(jnp.max(jnp.abs(values), axis=0, keepdims=True))
    out_ref[pl.ds(0, rows), :] = encode(values, scale)
    heads = jnp.broadcast_to(scale, (PAD, LANES))
    if far is None:
        out_ref[pl.ds(rows, PAD), :] = heads.astype(S32).astype(S16)
        return
    far_scale = column_scale(jnp.max(jnp.abs(far), axis=0, keepdims=True))
    out_ref[pl.ds(rows, PAD), :] = encode(far, far_scale)
    which = lax.broadcasted_iota(S32, (PAD, LANES), 0)
    heads = jnp.where(which == 0, heads, jnp.broadcast_to(far_scale, (PAD, LANES)))
    out_ref[pl.ds(rows + PAD, PAD), :] = heads.astype(S32).astype(S16)


def unpack_sum(refs, rows, has_far):
    total, far = None, None
    for ref in refs:
        heads = ref[pl.ds(rows + (PAD if has_far else 0), PAD), :].astype(S32).astype(F32)
        part = decode(ref[pl.ds(0, rows), :], heads[0:1])
        total = part if total is None else total + part
        if has_far:
            part = decode(ref[pl.ds(rows, PAD), :], heads[1:2])
            far = part if far is None else far + part
    return total, far


def halves(values):
    high = values.astype(BF16)
    return high, (values - high.astype(F32)).astype(BF16)


def sort_rows(matrix, values):
    high, low = halves(values)
    return jnp.dot(matrix, high, preferred_element_type=F32) + jnp.dot(matrix, low, preferred_element_type=F32)


def stage_kernel(order_ref, live_ref, tiles_ref, out_ref, arrived):
    def copy(p):
        return pltpu.make_async_copy(tiles_ref.at[order_ref[p]], out_ref.at[p], arrived.at[p])

    for p in range(tiles_ref.shape[0]):

        @pl.when(live_ref[p] > 0)
        def _():
            copy(p).start()

    for p in range(tiles_ref.shape[0]):

        @pl.when(live_ref[p] <= 0)
        def _():
            out_ref[p] = jnp.zeros(out_ref.shape[1:], out_ref.dtype)

    for p in range(tiles_ref.shape[0]):

        @pl.when(live_ref[p] > 0)
        def _():
            copy(p).wait()


def stage(tiles, order, live):
    smem = pl.BlockSpec(memory_space=pltpu.SMEM)
    tiles = pltpu.with_memory_space_constraint(tiles, pltpu.HBM)
    return pl.pallas_call(
        stage_kernel,
        out_shape=pltpu.VMEM(tiles.shape, tiles.dtype),
        in_specs=[smem, smem, pl.BlockSpec(memory_space=pl.ANY)],
        out_specs=pl.BlockSpec(memory_space=pltpu.VMEM),
        scratch_shapes=[pltpu.SemaphoreType.DMA((tiles.shape[0],))],
        compiler_params=pltpu.CompilerParams(vmem_limit_bytes=4 * 1024 * 1024),
        cost_estimate=pl.CostEstimate(flops=0, bytes_accessed=tiles.size * 2, transcendentals=0),
        name="stage",
    )(order, live, tiles)


def product_kernel(has_far, rows, place_ref, v_ref, rank_ref, *rest):
    amps, outs, (first, mates, table, raw) = rest[:2], rest[2:10], rest[10:]
    tiles, tile, _ = v_ref.shape
    steps = tiles // 4
    half = CW // 2
    groups = SIDE * SIDE
    peer = rows // groups

    y, core = place_ref[2], place_ref[3]
    depth = amps[0].shape[2]
    for k in range(SIDE):
        chip = lax.rem(y + SIDE - k, SIDE) * 2
        for c in range(2):
            at = (chip + (core if c == 0 else 1 - core)) * depth
            for j in range(4):
                table[pl.ds(pl.multiple_of(j * tile + at, depth), depth), :] = amps[c][k, j]

    def multiply(step, part):
        total = None
        for j in range(4):
            v = v_ref[step * 4 + j]
            t = table[j * tile : (j + 1) * tile, part * half : (part + 1) * half]
            add = jnp.dot(v, t, preferred_element_type=F32)
            total = add if total is None else total + add
        return total

    def sort(step, part, values):
        for b in range(tile // rows):
            block = step * (tile // rows) + b
            rank = rank_ref[part, pl.ds(block, 1), :]
            matrix = (lax.broadcasted_iota(S32, (rows, rows), 0) == rank).astype(F32).astype(BF16)
            done = sort_rows(matrix, values[b * rows : (b + 1) * rows])
            if part == 0:
                first[pl.ds(pl.multiple_of(block * rows, rows), rows), :] = done
            else:
                mates[pl.ds(block, 1)] = done.reshape(1, groups, peer, half)

    def columns(part):
        return pl.ds(part * half, half)

    for part in range(2):
        raw[pl.ds(0, tile), columns(part)] = multiply(0, part)

    def turn(step, carry):
        before = pl.multiple_of(lax.rem(step + 1, 2) * tile, tile)
        now = pl.multiple_of(lax.rem(step, 2) * tile, tile)
        held = [raw[pl.ds(before, tile), columns(part)] for part in range(2)]
        for part in range(2):
            total = multiply(step, part)
            sort(step - 1, part, held[part])
            raw[pl.ds(now, tile), columns(part)] = total
        return carry

    lax.fori_loop(1, steps, turn, 0)
    for part in range(2):
        sort(steps - 1, part, raw[pl.ds((steps - 1) % 2 * tile, tile), columns(part)])

    z, x = place_ref[0], place_ref[1]
    for kx in range(SIDE):
        for kz in range(SIDE):
            zt = lax.rem(z + kz, SIDE)
            xt = lax.rem(x + kx, SIDE)
            owner_id = zt * SIDE + xt
            base = pl.multiple_of(owner_id * rows, rows)
            far_parts = [None, None]
            sums = []
            for side in range(2):
                mine = first[pl.ds(base, rows), pl.ds(side * LANES, LANES)]
                other = mates[:, pl.ds(owner_id, 1), :, pl.ds(side * LANES, LANES)].reshape(rows, LANES)
                if has_far and side == 1:
                    far = other.T[LANES - NO // 2 :]
                    far_parts = [far[:, :LANES], far[:, LANES:]]
                    lane = lax.broadcasted_iota(S32, (rows, LANES), 1)
                    other = jnp.where(lane < LANES - NO // 2, other, 0.0)
                sums.append(mine + other)
            pack(outs[kx].at[zt], sums[0], far_parts[0])
            pack(outs[4 + kz].at[xt], sums[1], far_parts[1])


def packed_rows(rows, has_far):
    return rows + PAD * (2 if has_far else 1)


def product(integrals, amps, ranks, place, rows, has_far):
    tiles, tile, _ = integrals.shape
    groups = SIDE * SIDE
    half = CW // 2
    vmem, smem = pl.BlockSpec(memory_space=pltpu.VMEM), pl.BlockSpec(memory_space=pltpu.SMEM)
    out = (SIDE, packed_rows(rows, has_far), LANES)
    return pl.pallas_call(
        functools.partial(product_kernel, has_far, rows),
        out_shape=[jax.ShapeDtypeStruct(out, S16)] * 8,
        in_specs=[smem] + [vmem] * (2 + len(amps)),
        out_specs=[vmem] * 8,
        scratch_shapes=[
            pltpu.VMEM((groups * rows, half), F32),
            pltpu.VMEM((groups, groups, rows // groups, half), F32),
            pltpu.VMEM((4 * tile, CW), BF16),
            pltpu.VMEM((2 * tile, CW), F32),
        ],
        compiler_params=pltpu.CompilerParams(vmem_limit_bytes=VMEM),
        cost_estimate=pl.CostEstimate(
            flops=2 * tiles * tile * tile * CW, bytes_accessed=4 * tile * CW * 4, transcendentals=0
        ),
        name="product",
    )(place, integrals, ranks, *amps)


def chunk_rows(rows, far_flags):
    heights = [packed_rows(rows, flag) for flag in far_flags]
    return [(sum(heights[:c]), heights[c]) for c in range(len(heights))]


def relay_kernel(rows, far_flags, place_ref, *refs):
    count = 8 * len(far_flags)
    ins, outs = refs[:count], refs[count:]
    for c, (top, height) in enumerate(chunk_rows(rows, far_flags)):
        for side in range(2):
            for k in range(SIDE):
                at = lax.rem(place_ref[side] + k, SIDE)
                blocks = [r.at[at] for r in ins[c * 8 + side * 4 :][:4]]
                total, far = unpack_sum(blocks, rows, far_flags[c])
                pack(outs[side * 4 + k].at[pl.ds(top, height)], total, far)


def relay(pieces, place, rows, far_flags):
    height = sum(h for _, h in chunk_rows(rows, far_flags))
    vmem = pl.BlockSpec(memory_space=pltpu.VMEM)
    return pl.pallas_call(
        functools.partial(relay_kernel, rows, far_flags),
        out_shape=[jax.ShapeDtypeStruct((height, LANES), S16)] * 8,
        in_specs=[pl.BlockSpec(memory_space=pltpu.SMEM)] + [vmem] * len(pieces),
        out_specs=[vmem] * 8,
        compiler_params=pltpu.CompilerParams(vmem_limit_bytes=SMALL),
        name="relay",
    )(place, *pieces)


def owner_kernel(rows, far_flags, *refs):
    ins, own, send = refs[:8], refs[8], refs[9]
    for c, (top, height) in enumerate(chunk_rows(rows, far_flags)):
        has_far = far_flags[c]
        fars = []
        for side in range(2):
            blocks = [r.at[pl.ds(top, height)] for r in ins[side * 4 :][:4]]
            total, far = unpack_sum(blocks, rows, has_far)
            own[:, pl.ds((c * 2 + side) * LANES, LANES)] = total
            fars.append(far)
        if has_far:
            far = jnp.concatenate([jnp.zeros((LANES - NO // 2, rows), F32), jnp.concatenate(fars, axis=1)], axis=0)
            own[:, pl.ds(HALF, LANES)] = far.T
    scale = column_scale(jnp.max(jnp.abs(own[...]), axis=1, keepdims=True))
    send[:, pl.ds(0, HALF)] = encode(own[:, pl.ds(0, HALF)], scale)
    lane = lax.broadcasted_iota(S32, (rows, LANES), 1)
    far = jnp.round(own[:, pl.ds(HALF, LANES)] * (jnp.exp2(scale * (-1.0 / LOG_GRID)) * FULL))
    far = jnp.where(lane == 0, jnp.broadcast_to(scale, (rows, LANES)), far)
    send[:, pl.ds(HALF, LANES)] = far.astype(S32).astype(S16)


def owner(pieces, rows, far_flags):
    vmem = pl.BlockSpec(memory_space=pltpu.VMEM)
    width = HALF + LANES
    return pl.pallas_call(
        functools.partial(owner_kernel, rows, far_flags),
        out_shape=[jax.ShapeDtypeStruct((rows, width), F32), jax.ShapeDtypeStruct((rows, width), S16)],
        in_specs=[vmem] * len(pieces),
        out_specs=[vmem] * 2,
        compiler_params=pltpu.CompilerParams(vmem_limit_bytes=SMALL),
        name="owner",
    )(*pieces)


def close_kernel(rows, own, came, ranks, energy, pair_sum, spread, out, joined):
    heads = came[:, pl.ds(HALF, LANES)].astype(S32).astype(F32)
    scale = jnp.exp2(heads[:, 0:1] * (1.0 / LOG_GRID)) * (1.0 / FULL)
    plain = came[...].astype(S32).astype(F32) * scale
    slot = lax.broadcasted_iota(S32, (rows, rows), 1)
    back = [(slot == ranks[:, k : k + 1]).astype(F32).astype(BF16) for k in range(2)]
    mine = sort_rows(back[0], own[...])
    other = sort_rows(back[1], plain)
    lane = lax.broadcasted_iota(S32, (rows, LANES), 1)
    off_diagonal = lane < LANES - NO // 2
    edge = HALF - LANES
    joined[:, pl.ds(0, edge)] = mine[:, :edge]
    joined[:, pl.ds(HALF, edge)] = other[:, :edge]
    last_mine, last_other = mine[:, edge:HALF], other[:, edge:HALF]
    joined[:, pl.ds(edge, LANES)] = last_mine + jnp.where(off_diagonal, 0.0, last_other)
    joined[:, pl.ds(HALF + edge, LANES)] = jnp.where(off_diagonal, last_other, mine[:, HALF:] + other[:, HALF:])
    total = None
    for part in halves(joined[...]):
        add = jnp.dot(part, spread[...], preferred_element_type=F32)
        total = add if total is None else total + add
    out[...] = total / (energy[...] - pair_sum[...])


def close(own, came, ranks, energy, pair_sum, spread, rows):
    vmem = pl.BlockSpec(memory_space=pltpu.VMEM)
    return pl.pallas_call(
        functools.partial(close_kernel, rows),
        out_shape=jax.ShapeDtypeStruct((rows, OCC), F32),
        in_specs=[vmem] * 6,
        out_specs=vmem,
        scratch_shapes=[pltpu.VMEM((rows, OCC), F32)],
        compiler_params=pltpu.CompilerParams(vmem_limit_bytes=SMALL),
        name="close",
    )(own, came, ranks, energy, pair_sum, spread)


def shifted(dz, dx):
    return [
        (z * SIDE + x, (z + dz) % SIDE * SIDE + (x + dx) % SIDE) for z in range(SIDE) for x in range(SIDE)
    ]


def spread_out(pieces, across_x_first):
    got = list(pieces)
    for k in (2, 1, 3):
        for side in range(2):
            along_x = (side == 0) == across_x_first
            perm = shifted(0, k) if along_x else shifted(k, 0)
            got[side * 4 + k] = lax.ppermute(pieces[side * 4 + k], "col", perm)
    return got


def shifted_rows(dy, dcore):
    return [(y * 2 + c, (y + dy) % SIDE * 2 + (c + dcore) % 2) for y in range(SIDE) for c in range(2)]


def fetch_along(part):
    return [part] + [lax.ppermute(part, "row", shifted_rows(k, 0)) for k in range(1, SIDE)]


def share(along):
    mine = jnp.stack(along)
    return [mine, lax.ppermute(mine, "row", shifted_rows(0, 1))]


def body(integrals, tile_count, tile_list, amplitudes, pair_energy, occ_energy, partner):
    rows = partner.shape[0]
    groups = SIDE * SIDE
    first, mates_of = pair_orders()
    half = CW // 2
    column_order = np.concatenate(
        [np.concatenate([first[c * half :][:half], mates_of[c * half :][:half]]) for c in range(CHUNKS)]
    )
    pair_ids = jnp.arange(OCC, dtype=S32)
    sort = (pair_ids[:, None] == jnp.asarray(column_order)[None, :]).astype(BF16)
    spread = (jnp.asarray(np.concatenate([first, mates_of]))[:, None] == pair_ids[None, :]).astype(BF16)

    blocks, depth, _ = amplitudes.shape
    sorted_amp = jnp.dot(amplitudes.reshape(blocks * depth, OCC), sort, preferred_element_type=F32).astype(BF16)
    parts = [sorted_amp[:, c * CW : (c + 1) * CW].reshape(blocks, depth, CW) for c in range(CHUNKS)]

    peer = rows // groups
    target = partner // rows % groups
    key_local = partner % rows
    row_ids = jnp.arange(rows, dtype=S32)
    same_target = target[:, None] == target[None, :]
    own_rank = target * peer + jnp.sum(same_target & (row_ids[None, :] < row_ids[:, None]), axis=1)
    mate_rank = target * peer + jnp.sum(same_target & (key_local[None, :] < key_local[:, None]), axis=1)
    both = jnp.concatenate([own_rank, mate_rank]).astype(S32)
    spoken = jnp.broadcast_to(both[None, :], (groups, 2 * rows))
    ranks = lax.all_to_all(spoken, "col", split_axis=0, concat_axis=0, tiled=True)
    along = [fetch_along(part) for part in parts]
    ranks, along[0] = lax.optimization_barrier((ranks, along[0]))
    ranks = jnp.stack([ranks[:, :rows], ranks[:, rows:]])

    col = lax.axis_index("col")
    row = lax.axis_index("row")
    place = jnp.stack([col // SIDE, col % SIDE, row // 2, row % 2]).astype(S32)
    slots = tile_list[0, 0]
    slot_ids = jnp.arange(slots.shape[0], dtype=S32)
    order = jnp.sum(jnp.where(slots[None, :] == slot_ids[:, None], slot_ids[None, :], 0), axis=1)
    live = (order < tile_count[0, 0]).astype(S32)

    tiles = stage(integrals[0, 0], order, live)
    far_flags = tuple(c == CHUNKS - 1 for c in range(CHUNKS))
    landed = []
    for c in range(CHUNKS):
        sent = product(tiles, share(along[c]), ranks, place, rows, far_flags[c])
        if c + 1 < CHUNKS:
            sent, along[c + 1] = lax.optimization_barrier((sent, along[c + 1]))
        landed += spread_out(sent, True)
    landed = spread_out(relay(landed, place, rows, far_flags), False)
    own, send = owner(landed, rows, far_flags)
    came = lax.all_to_all(send, "col", split_axis=0, concat_axis=0, tiled=True)
    pair_sum = (occ_energy[:, None] + occ_energy[None, :]).reshape(1, OCC)
    back = jnp.stack([own_rank, mate_rank], axis=1).astype(S32)
    return close(own, came, back, pair_energy[:, None], pair_sum, spread, rows)


def solution(mesh):
    return jax.shard_map(
        body,
        mesh=mesh,
        in_specs=(
            P("row", "col", None, None, None),
            P("row", "col"),
            P("row", "col", None),
            P("col", "row", None),
            P(("row", "col")),
            P(),
            P(("row", "col")),
        ),
        out_specs=P(("row", "col"), None),
        check_vma=False,
    )
```

```python
import functools

import numpy as np
import jax
import jax.numpy as jnp
from jax import lax
from jax.experimental import pallas as pl
from jax.experimental.pallas import tpu as pltpu
from jax.sharding import PartitionSpec as P

F32, S32, S16, BF16 = jnp.float32, jnp.int32, jnp.int16, jnp.bfloat16
NO = 32
OCC = NO * NO
HALF = OCC // 2
CHUNKS = 2
CW = OCC // CHUNKS
LANES = 128
SIDE = 4
PAD = 16
LOG_GRID = 200.0
FULL = 32760.0
TINY = 1e-37
VMEM = 20 * 1024 * 1024
SMALL = 16 * 1024 * 1024


def pair_orders():
    first, mates = [], []
    for gap in range(1, NO // 2 + 1):
        for i in range(NO if gap < NO // 2 else NO // 2):
            j = (i + gap) % NO
            first.append(i * NO + j)
            mates.append(j * NO + i)
    first += [i * NO + i for i in range(NO // 2)]
    mates += [i * NO + i for i in range(NO // 2, NO)]
    return np.array(first, np.int32), np.array(mates, np.int32)


def column_scale(level):
    return jnp.ceil(jnp.log(jnp.maximum(level, TINY)) * (LOG_GRID / float(np.log(2.0))))


def encode(values, scale):
    return jnp.round(values * (jnp.exp2(scale * (-1.0 / LOG_GRID)) * FULL)).astype(S32).astype(S16)


def decode(coded, scale):
    return coded.astype(S32).astype(F32) * (jnp.exp2(scale * (1.0 / LOG_GRID)) * (1.0 / FULL))


def pack(out_ref, values, far):
    rows = values.shape[0]
    scale = column_scale(jnp.max(jnp.abs(values), axis=0, keepdims=True))
    out_ref[pl.ds(0, rows), :] = encode(values, scale)
    heads = jnp.broadcast_to(scale, (PAD, LANES))
    if far is None:
        out_ref[pl.ds(rows, PAD), :] = heads.astype(S32).astype(S16)
        return
    far_scale = column_scale(jnp.max(jnp.abs(far), axis=0, keepdims=True))
    out_ref[pl.ds(rows, PAD), :] = encode(far, far_scale)
    which = lax.broadcasted_iota(S32, (PAD, LANES), 0)
    heads = jnp.where(which == 0, heads, jnp.broadcast_to(far_scale, (PAD, LANES)))
    out_ref[pl.ds(rows + PAD, PAD), :] = heads.astype(S32).astype(S16)


def unpack_sum(refs, rows, has_far):
    total, far = None, None
    for ref in refs:
        heads = ref[pl.ds(rows + (PAD if has_far else 0), PAD), :].astype(S32).astype(F32)
        part = decode(ref[pl.ds(0, rows), :], heads[0:1])
        total = part if total is None else total + part
        if has_far:
            part = decode(ref[pl.ds(rows, PAD), :], heads[1:2])
            far = part if far is None else far + part
    return total, far


def halves(values):
    high = values.astype(BF16)
    return high, (values - high.astype(F32)).astype(BF16)


def sort_rows(matrix, values):
    high, low = halves(values)
    return jnp.dot(matrix, high, preferred_element_type=F32) + jnp.dot(matrix, low, preferred_element_type=F32)


def stage_kernel(order_ref, live_ref, tiles_ref, out_ref, arrived):
    def copy(p):
        return pltpu.make_async_copy(tiles_ref.at[order_ref[p]], out_ref.at[p], arrived.at[p])

    for p in range(tiles_ref.shape[0]):

        @pl.when(live_ref[p] > 0)
        def _():
            copy(p).start()

    for p in range(tiles_ref.shape[0]):

        @pl.when(live_ref[p] <= 0)
        def _():
            out_ref[p] = jnp.zeros(out_ref.shape[1:], out_ref.dtype)

    for p in range(tiles_ref.shape[0]):

        @pl.when(live_ref[p] > 0)
        def _():
            copy(p).wait()


def stage(tiles, order, live):
    smem = pl.BlockSpec(memory_space=pltpu.SMEM)
    tiles = pltpu.with_memory_space_constraint(tiles, pltpu.HBM)
    return pl.pallas_call(
        stage_kernel,
        out_shape=pltpu.VMEM(tiles.shape, tiles.dtype),
        in_specs=[smem, smem, pl.BlockSpec(memory_space=pl.ANY)],
        out_specs=pl.BlockSpec(memory_space=pltpu.VMEM),
        scratch_shapes=[pltpu.SemaphoreType.DMA((tiles.shape[0],))],
        compiler_params=pltpu.CompilerParams(vmem_limit_bytes=4 * 1024 * 1024),
        cost_estimate=pl.CostEstimate(flops=0, bytes_accessed=tiles.size * 2, transcendentals=0),
        name="stage",
    )(order, live, tiles)


def product_kernel(has_far, rows, place_ref, v_ref, rank_ref, *rest):
    amps, outs, (first, mates, table, raw) = rest[:2], rest[2:10], rest[10:]
    tiles, tile, _ = v_ref.shape
    steps = tiles // 4
    half = CW // 2
    groups = SIDE * SIDE
    peer = rows // groups

    z, x, y, core = place_ref[0], place_ref[1], place_ref[2], place_ref[3]
    depth = amps[0].shape[2]
    for k in range(SIDE):
        chip = lax.rem(y + SIDE - k, SIDE) * 2
        for c in range(2):
            at = (chip + (core if c == 0 else 1 - core)) * depth
            for j in range(4):
                table[pl.ds(pl.multiple_of(j * tile + at, depth), depth), :] = amps[c][k, j]

    def relative(block):
        return lax.rem(z + SIDE - block // SIDE, SIDE) * SIDE + lax.rem(x + SIDE - lax.rem(block, SIDE), SIDE)

    def multiply(step, part):
        total = None
        for j in range(4):
            v = v_ref[step * 4 + j]
            t = table[j * tile : (j + 1) * tile, part * half : (part + 1) * half]
            add = jnp.dot(v, t, preferred_element_type=F32)
            total = add if total is None else total + add
        return total

    def sort(step, part, values):
        for b in range(tile // rows):
            block = step * (tile // rows) + b
            rank = rank_ref[part, pl.ds(relative(block), 1), :]
            matrix = (lax.broadcasted_iota(S32, (rows, rows), 0) == rank).astype(F32).astype(BF16)
            done = sort_rows(matrix, values[b * rows : (b + 1) * rows])
            if part == 0:
                first[pl.ds(pl.multiple_of(block * rows, rows), rows), :] = done
            else:
                mates[pl.ds(block, 1)] = done.reshape(1, groups, peer, half)

    def columns(part):
        return pl.ds(part * half, half)

    for part in range(2):
        raw[pl.ds(0, tile), columns(part)] = multiply(0, part)

    def turn(step, carry):
        before = pl.multiple_of(lax.rem(step + 1, 2) * tile, tile)
        now = pl.multiple_of(lax.rem(step, 2) * tile, tile)
        held = [raw[pl.ds(before, tile), columns(part)] for part in range(2)]
        for part in range(2):
            total = multiply(step, part)
            sort(step - 1, part, held[part])
            raw[pl.ds(now, tile), columns(part)] = total
        return carry

    lax.fori_loop(1, steps, turn, 0)
    for part in range(2):
        sort(steps - 1, part, raw[pl.ds((steps - 1) % 2 * tile, tile), columns(part)])

    for kx in range(SIDE):
        for kz in range(SIDE):
            zt = lax.rem(z + kz, SIDE)
            xt = lax.rem(x + kx, SIDE)
            owner_id = zt * SIDE + xt
            base = pl.multiple_of(owner_id * rows, rows)
            far_parts = [None, None]
            sums = []
            for side in range(2):
                mine = first[pl.ds(base, rows), pl.ds(side * LANES, LANES)]
                other = mates[:, pl.ds(owner_id, 1), :, pl.ds(side * LANES, LANES)].reshape(rows, LANES)
                if has_far and side == 1:
                    far = other.T[LANES - NO // 2 :]
                    far_parts = [far[:, :LANES], far[:, LANES:]]
                    lane = lax.broadcasted_iota(S32, (rows, LANES), 1)
                    other = jnp.where(lane < LANES - NO // 2, other, 0.0)
                sums.append(mine + other)
            pack(outs[kx].at[zt], sums[0], far_parts[0])
            pack(outs[4 + kz].at[xt], sums[1], far_parts[1])


def packed_rows(rows, has_far):
    return rows + PAD * (2 if has_far else 1)


def product(integrals, amps, ranks, place, rows, has_far):
    tiles, tile, _ = integrals.shape
    groups = SIDE * SIDE
    half = CW // 2
    vmem, smem = pl.BlockSpec(memory_space=pltpu.VMEM), pl.BlockSpec(memory_space=pltpu.SMEM)
    out = (SIDE, packed_rows(rows, has_far), LANES)
    return pl.pallas_call(
        functools.partial(product_kernel, has_far, rows),
        out_shape=[jax.ShapeDtypeStruct(out, S16)] * 8,
        in_specs=[smem] + [vmem] * (2 + len(amps)),
        out_specs=[vmem] * 8,
        scratch_shapes=[
            pltpu.VMEM((groups * rows, half), F32),
            pltpu.VMEM((groups, groups, rows // groups, half), F32),
            pltpu.VMEM((4 * tile, CW), BF16),
            pltpu.VMEM((2 * tile, CW), F32),
        ],
        compiler_params=pltpu.CompilerParams(vmem_limit_bytes=VMEM),
        cost_estimate=pl.CostEstimate(
            flops=2 * tiles * tile * tile * CW, bytes_accessed=4 * tile * CW * 4, transcendentals=0
        ),
        name="product",
    )(place, integrals, ranks, *amps)


def chunk_rows(rows, far_flags):
    heights = [packed_rows(rows, flag) for flag in far_flags]
    return [(sum(heights[:c]), heights[c]) for c in range(len(heights))]


def relay_kernel(rows, far_flags, place_ref, *refs):
    count = 8 * len(far_flags)
    ins, outs = refs[:count], refs[count:]
    for c, (top, height) in enumerate(chunk_rows(rows, far_flags)):
        for side in range(2):
            for k in range(SIDE):
                at = lax.rem(place_ref[side] + k, SIDE)
                blocks = [r.at[at] for r in ins[c * 8 + side * 4 :][:4]]
                total, far = unpack_sum(blocks, rows, far_flags[c])
                pack(outs[side * 4 + k].at[pl.ds(top, height)], total, far)


def relay(pieces, place, rows, far_flags):
    height = sum(h for _, h in chunk_rows(rows, far_flags))
    vmem = pl.BlockSpec(memory_space=pltpu.VMEM)
    return pl.pallas_call(
        functools.partial(relay_kernel, rows, far_flags),
        out_shape=[jax.ShapeDtypeStruct((height, LANES), S16)] * 8,
        in_specs=[pl.BlockSpec(memory_space=pltpu.SMEM)] + [vmem] * len(pieces),
        out_specs=[vmem] * 8,
        compiler_params=pltpu.CompilerParams(vmem_limit_bytes=SMALL),
        name="relay",
    )(place, *pieces)


def owner_kernel(rows, far_flags, *refs):
    ins, own, send = refs[:8], refs[8], refs[9]
    for c, (top, height) in enumerate(chunk_rows(rows, far_flags)):
        has_far = far_flags[c]
        fars = []
        for side in range(2):
            blocks = [r.at[pl.ds(top, height)] for r in ins[side * 4 :][:4]]
            total, far = unpack_sum(blocks, rows, has_far)
            own[:, pl.ds((c * 2 + side) * LANES, LANES)] = total
            fars.append(far)
        if has_far:
            far = jnp.concatenate([jnp.zeros((LANES - NO // 2, rows), F32), jnp.concatenate(fars, axis=1)], axis=0)
            own[:, pl.ds(HALF, LANES)] = far.T
    scale = column_scale(jnp.max(jnp.abs(own[...]), axis=1, keepdims=True))
    send[:, pl.ds(0, HALF)] = encode(own[:, pl.ds(0, HALF)], scale)
    lane = lax.broadcasted_iota(S32, (rows, LANES), 1)
    far = jnp.round(own[:, pl.ds(HALF, LANES)] * (jnp.exp2(scale * (-1.0 / LOG_GRID)) * FULL))
    far = jnp.where(lane == 0, jnp.broadcast_to(scale, (rows, LANES)), far)
    send[:, pl.ds(HALF, LANES)] = far.astype(S32).astype(S16)


def owner(pieces, rows, far_flags):
    vmem = pl.BlockSpec(memory_space=pltpu.VMEM)
    width = HALF + LANES
    return pl.pallas_call(
        functools.partial(owner_kernel, rows, far_flags),
        out_shape=[jax.ShapeDtypeStruct((rows, width), F32), jax.ShapeDtypeStruct((rows, width), S16)],
        in_specs=[vmem] * len(pieces),
        out_specs=[vmem] * 2,
        compiler_params=pltpu.CompilerParams(vmem_limit_bytes=SMALL),
        name="owner",
    )(*pieces)


def close_kernel(rows, own, came, ranks, energy, pair_sum, spread, out, joined):
    heads = came[:, pl.ds(HALF, LANES)].astype(S32).astype(F32)
    scale = jnp.exp2(heads[:, 0:1] * (1.0 / LOG_GRID)) * (1.0 / FULL)
    plain = came[...].astype(S32).astype(F32) * scale
    slot = lax.broadcasted_iota(S32, (rows, rows), 1)
    back = [(slot == ranks[:, k : k + 1]).astype(F32).astype(BF16) for k in range(2)]
    mine = sort_rows(back[0], own[...])
    other = sort_rows(back[1], plain)
    lane = lax.broadcasted_iota(S32, (rows, LANES), 1)
    off_diagonal = lane < LANES - NO // 2
    edge = HALF - LANES
    joined[:, pl.ds(0, edge)] = mine[:, :edge]
    joined[:, pl.ds(HALF, edge)] = other[:, :edge]
    last_mine, last_other = mine[:, edge:HALF], other[:, edge:HALF]
    joined[:, pl.ds(edge, LANES)] = last_mine + jnp.where(off_diagonal, 0.0, last_other)
    joined[:, pl.ds(HALF + edge, LANES)] = jnp.where(off_diagonal, last_other, mine[:, HALF:] + other[:, HALF:])
    total = None
    for part in halves(joined[...]):
        add = jnp.dot(part, spread[...], preferred_element_type=F32)
        total = add if total is None else total + add
    out[...] = total / (energy[...] - pair_sum[...])


def close(own, came, ranks, energy, pair_sum, spread, rows):
    vmem = pl.BlockSpec(memory_space=pltpu.VMEM)
    return pl.pallas_call(
        functools.partial(close_kernel, rows),
        out_shape=jax.ShapeDtypeStruct((rows, OCC), F32),
        in_specs=[vmem] * 6,
        out_specs=vmem,
        scratch_shapes=[pltpu.VMEM((rows, OCC), F32)],
        compiler_params=pltpu.CompilerParams(vmem_limit_bytes=SMALL),
        name="close",
    )(own, came, ranks, energy, pair_sum, spread)


def shifted(dz, dx):
    return [
        (z * SIDE + x, (z + dz) % SIDE * SIDE + (x + dx) % SIDE) for z in range(SIDE) for x in range(SIDE)
    ]


def spread_out(pieces, across_x_first):
    got = list(pieces)
    for k in (2, 1, 3):
        for side in range(2):
            along_x = (side == 0) == across_x_first
            perm = shifted(0, k) if along_x else shifted(k, 0)
            got[side * 4 + k] = lax.ppermute(pieces[side * 4 + k], "col", perm)
    return got


def shifted_rows(dy, dcore):
    return [(y * 2 + c, (y + dy) % SIDE * 2 + (c + dcore) % 2) for y in range(SIDE) for c in range(2)]


def fetch_along(part):
    return [part] + [lax.ppermute(part, "row", shifted_rows(k, 0)) for k in range(1, SIDE)]


def share(along):
    mine = jnp.stack(along)
    return [mine, lax.ppermute(mine, "row", shifted_rows(0, 1))]


def body(integrals, tile_count, tile_list, amplitudes, pair_energy, occ_energy, partner):
    rows = partner.shape[0]
    groups = SIDE * SIDE
    first, mates_of = pair_orders()
    half = CW // 2
    column_order = np.concatenate(
        [np.concatenate([first[c * half :][:half], mates_of[c * half :][:half]]) for c in range(CHUNKS)]
    )
    pair_ids = jnp.arange(OCC, dtype=S32)
    sort = (pair_ids[:, None] == jnp.asarray(column_order)[None, :]).astype(BF16)
    spread = (jnp.asarray(np.concatenate([first, mates_of]))[:, None] == pair_ids[None, :]).astype(BF16)

    blocks, depth, _ = amplitudes.shape
    sorted_amp = jnp.dot(amplitudes.reshape(blocks * depth, OCC), sort, preferred_element_type=F32).astype(BF16)
    parts = [sorted_amp[:, c * CW : (c + 1) * CW].reshape(blocks, depth, CW) for c in range(CHUNKS)]

    peer = rows // groups
    target = partner // rows % groups
    key_local = partner % rows
    row_ids = jnp.arange(rows, dtype=S32)
    same_target = target[:, None] == target[None, :]
    own_rank = target * peer + jnp.sum(same_target & (row_ids[None, :] < row_ids[:, None]), axis=1)
    mate_rank = target * peer + jnp.sum(same_target & (key_local[None, :] < key_local[:, None]), axis=1)
    both = jnp.concatenate([own_rank, mate_rank]).astype(S32)
    def fetch_across(part, step):
        return jnp.concatenate([part] + [lax.ppermute(part, "col", step(k)) for k in range(1, SIDE)])

    along = [fetch_along(part) for part in parts]
    ranks = fetch_across(both.reshape(1, 2, rows), lambda k: shifted(0, k))
    ranks, along[0] = lax.optimization_barrier((ranks, along[0]))
    ranks = jnp.swapaxes(fetch_across(ranks, lambda k: shifted(k, 0)), 0, 1)

    col = lax.axis_index("col")
    row = lax.axis_index("row")
    place = jnp.stack([col // SIDE, col % SIDE, row // 2, row % 2]).astype(S32)
    slots = tile_list[0, 0]
    slot_ids = jnp.arange(slots.shape[0], dtype=S32)
    order = jnp.sum(jnp.where(slots[None, :] == slot_ids[:, None], slot_ids[None, :], 0), axis=1)
    live = (order < tile_count[0, 0]).astype(S32)

    tiles = stage(integrals[0, 0], order, live)
    far_flags = tuple(c == CHUNKS - 1 for c in range(CHUNKS))
    landed = []
    for c in range(CHUNKS):
        sent = product(tiles, share(along[c]), ranks, place, rows, far_flags[c])
        if c > 0:
            sent, landed = lax.optimization_barrier((sent, landed))
        if c + 1 < CHUNKS:
            sent, along[c + 1] = lax.optimization_barrier((sent, along[c + 1]))
        landed += spread_out(sent, True)
    landed = spread_out(relay(landed, place, rows, far_flags), False)
    own, send = owner(landed, rows, far_flags)
    came = lax.all_to_all(send, "col", split_axis=0, concat_axis=0, tiled=True)
    pair_sum = (occ_energy[:, None] + occ_energy[None, :]).reshape(1, OCC)
    back = jnp.stack([own_rank, mate_rank], axis=1).astype(S32)
    return close(own, came, back, pair_energy[:, None], pair_sum, spread, rows)


def solution(mesh):
    return jax.shard_map(
        body,
        mesh=mesh,
        in_specs=(
            P("row", "col", None, None, None),
            P("row", "col"),
            P("row", "col", None),
            P("col", "row", None),
            P(("row", "col")),
            P(),
            P(("row", "col")),
        ),
        out_specs=P(("row", "col"), None),
        check_vma=False,
    )
```

```python
import functools

import numpy as np
import jax
import jax.numpy as jnp
from jax import lax
from jax.experimental import pallas as pl
from jax.experimental.pallas import tpu as pltpu
from jax.sharding import PartitionSpec as P

F32, S32, S16, BF16 = jnp.float32, jnp.int32, jnp.int16, jnp.bfloat16
NO = 32
OCC = NO * NO
HALF = OCC // 2
CHUNKS = 2
CW = OCC // CHUNKS
LANES = 128
SIDE = 4
PAD = 16
LOG_GRID = 200.0
FULL = 32760.0
TINY = 1e-37
VMEM = 20 * 1024 * 1024
SMALL = 16 * 1024 * 1024


def pair_orders():
    first, mates = [], []
    for gap in range(1, NO // 2 + 1):
        for i in range(NO if gap < NO // 2 else NO // 2):
            j = (i + gap) % NO
            first.append(i * NO + j)
            mates.append(j * NO + i)
    first += [i * NO + i for i in range(NO // 2)]
    mates += [i * NO + i for i in range(NO // 2, NO)]
    return np.array(first, np.int32), np.array(mates, np.int32)


def column_scale(level):
    return jnp.ceil(jnp.log(jnp.maximum(level, TINY)) * (LOG_GRID / float(np.log(2.0))))


def encode(values, scale):
    return jnp.round(values * (jnp.exp2(scale * (-1.0 / LOG_GRID)) * FULL)).astype(S32).astype(S16)


def decode(coded, scale):
    return coded.astype(S32).astype(F32) * (jnp.exp2(scale * (1.0 / LOG_GRID)) * (1.0 / FULL))


def pack(out_ref, values, far):
    rows, wide = values.shape
    scale = column_scale(jnp.max(jnp.abs(values), axis=0, keepdims=True))
    out_ref[pl.ds(0, rows), :] = encode(values, scale)
    heads = jnp.broadcast_to(scale, (PAD, wide))
    if far is None:
        out_ref[pl.ds(rows, PAD), :] = heads.astype(S32).astype(S16)
        return
    far_scale = column_scale(jnp.max(jnp.abs(far), axis=0, keepdims=True))
    out_ref[pl.ds(rows, PAD), :] = encode(far, far_scale)
    which = lax.broadcasted_iota(S32, (PAD, wide), 0)
    heads = jnp.where(which == 0, heads, jnp.broadcast_to(far_scale, (PAD, wide)))
    out_ref[pl.ds(rows + PAD, PAD), :] = heads.astype(S32).astype(S16)


def unpack_sum(refs, rows, has_far):
    total, far = None, None
    for ref in refs:
        heads = ref[pl.ds(rows + (PAD if has_far else 0), PAD), :].astype(S32).astype(F32)
        part = decode(ref[pl.ds(0, rows), :], heads[0:1])
        total = part if total is None else total + part
        if has_far:
            part = decode(ref[pl.ds(rows, PAD), :], heads[1:2])
            far = part if far is None else far + part
    return total, far


def halves(values):
    high = values.astype(BF16)
    return high, (values - high.astype(F32)).astype(BF16)


def sort_rows(matrix, values):
    high, low = halves(values)
    return jnp.dot(matrix, high, preferred_element_type=F32) + jnp.dot(matrix, low, preferred_element_type=F32)


def stage_kernel(order_ref, live_ref, tiles_ref, out_ref, arrived):
    def copy(p):
        return pltpu.make_async_copy(tiles_ref.at[order_ref[p]], out_ref.at[p], arrived.at[p])

    for p in range(tiles_ref.shape[0]):

        @pl.when(live_ref[p] > 0)
        def _():
            copy(p).start()

    for p in range(tiles_ref.shape[0]):

        @pl.when(live_ref[p] <= 0)
        def _():
            out_ref[p] = jnp.zeros(out_ref.shape[1:], out_ref.dtype)

    for p in range(tiles_ref.shape[0]):

        @pl.when(live_ref[p] > 0)
        def _():
            copy(p).wait()


def stage(tiles, order, live):
    smem = pl.BlockSpec(memory_space=pltpu.SMEM)
    tiles = pltpu.with_memory_space_constraint(tiles, pltpu.HBM)
    return pl.pallas_call(
        stage_kernel,
        out_shape=pltpu.VMEM(tiles.shape, tiles.dtype),
        in_specs=[smem, smem, pl.BlockSpec(memory_space=pl.ANY)],
        out_specs=pl.BlockSpec(memory_space=pltpu.VMEM),
        scratch_shapes=[pltpu.SemaphoreType.DMA((tiles.shape[0],))],
        compiler_params=pltpu.CompilerParams(vmem_limit_bytes=4 * 1024 * 1024),
        cost_estimate=pl.CostEstimate(flops=0, bytes_accessed=tiles.size * 2, transcendentals=0),
        name="stage",
    )(order, live, tiles)


def product_kernel(has_far, rows, place_ref, v_ref, rank_ref, *rest):
    amps, outs, (first, mates, table, raw) = rest[:2], rest[2:6], rest[6:]
    tiles, tile, _ = v_ref.shape
    steps = tiles // 4
    half = CW // 2
    groups = SIDE * SIDE
    peer = rows // groups

    y, core, here, there = (place_ref[k] for k in range(4))
    depth = amps[0].shape[2]
    for k in range(SIDE):
        chip = lax.rem(y + SIDE - k, SIDE) * 2
        for c in range(2):
            at = (chip + (core if c == 0 else 1 - core)) * depth
            for j in range(4):
                table[pl.ds(pl.multiple_of(j * tile + at, depth), depth), :] = amps[c][k, j]

    def multiply(step, part):
        total = None
        for j in range(4):
            v = v_ref[step * 4 + j]
            t = table[j * tile : (j + 1) * tile, part * half : (part + 1) * half]
            add = jnp.dot(v, t, preferred_element_type=F32)
            total = add if total is None else total + add
        return total

    def sort(step, part, values):
        for b in range(tile // rows):
            block = step * (tile // rows) + b
            rank = rank_ref[part, pl.ds(block, 1), :]
            matrix = (lax.broadcasted_iota(S32, (rows, rows), 0) == rank).astype(F32).astype(BF16)
            done = sort_rows(matrix, values[b * rows : (b + 1) * rows])
            if part == 0:
                first[pl.ds(pl.multiple_of(block * rows, rows), rows), :] = done
            else:
                mates[pl.ds(block, 1)] = done.reshape(1, groups, peer, half)

    def columns(part):
        return pl.ds(part * half, half)

    for part in range(2):
        raw[pl.ds(0, tile), columns(part)] = multiply(0, part)

    def turn(step, carry):
        before = pl.multiple_of(lax.rem(step + 1, 2) * tile, tile)
        now = pl.multiple_of(lax.rem(step, 2) * tile, tile)
        held = [raw[pl.ds(before, tile), columns(part)] for part in range(2)]
        for part in range(2):
            total = multiply(step, part)
            sort(step - 1, part, held[part])
            raw[pl.ds(now, tile), columns(part)] = total
        return carry

    lax.fori_loop(1, steps, turn, 0)
    for part in range(2):
        sort(steps - 1, part, raw[pl.ds((steps - 1) % 2 * tile, tile), columns(part)])

    for k in range(SIDE):
        for m in range(SIDE):
            near, later = lax.rem(here + k, SIDE), lax.rem(there + m, SIDE)
            owner_id = jnp.where(core == 0, later * SIDE + near, near * SIDE + later)
            base = pl.multiple_of(owner_id * rows, rows)
            mine = first[pl.ds(base, rows), :]
            other = mates[:, pl.ds(owner_id, 1)].reshape(rows, half)
            far = None
            if has_far:
                far = other[:, half - LANES :].T[LANES - NO // 2 :]
                lane = lax.broadcasted_iota(S32, (rows, half), 1)
                other = jnp.where(lane < half - NO // 2, other, 0.0)
            pack(outs[k].at[m], mine + other, far)


def packed_rows(rows, has_far):
    return rows + PAD * (2 if has_far else 1)


def product(integrals, amps, ranks, place, rows, has_far):
    tiles, tile, _ = integrals.shape
    groups = SIDE * SIDE
    half = CW // 2
    vmem, smem = pl.BlockSpec(memory_space=pltpu.VMEM), pl.BlockSpec(memory_space=pltpu.SMEM)
    out = (SIDE, packed_rows(rows, has_far), half)
    return pl.pallas_call(
        functools.partial(product_kernel, has_far, rows),
        out_shape=[jax.ShapeDtypeStruct(out, S16)] * SIDE,
        in_specs=[smem] + [vmem] * (2 + len(amps)),
        out_specs=[vmem] * SIDE,
        scratch_shapes=[
            pltpu.VMEM((groups * rows, half), F32),
            pltpu.VMEM((groups, groups, rows // groups, half), F32),
            pltpu.VMEM((4 * tile, CW), BF16),
            pltpu.VMEM((2 * tile, CW), F32),
        ],
        compiler_params=pltpu.CompilerParams(vmem_limit_bytes=VMEM),
        cost_estimate=pl.CostEstimate(
            flops=2 * tiles * tile * tile * CW, bytes_accessed=4 * tile * CW * 4, transcendentals=0
        ),
        name="product",
    )(place, integrals, ranks, *amps)


def chunk_rows(rows, far_flags):
    heights = [packed_rows(rows, flag) for flag in far_flags]
    return [(sum(heights[:c]), heights[c]) for c in range(len(heights))]


def relay_kernel(rows, far_flags, *refs):
    ins, outs = refs[:-SIDE], refs[-SIDE:]
    for c, (top, height) in enumerate(chunk_rows(rows, far_flags)):
        for m in range(SIDE):
            blocks = [r.at[m] for r in ins[c * SIDE :][:SIDE]]
            total, far = unpack_sum(blocks, rows, far_flags[c])
            pack(outs[m].at[pl.ds(top, height)], total, far)


def relay(came, rows, far_flags):
    height = sum(h for _, h in chunk_rows(rows, far_flags))
    vmem = pl.BlockSpec(memory_space=pltpu.VMEM)
    return pl.pallas_call(
        functools.partial(relay_kernel, rows, far_flags),
        out_shape=[jax.ShapeDtypeStruct((height, CW // 2), S16)] * SIDE,
        in_specs=[vmem] * len(came),
        out_specs=[vmem] * SIDE,
        compiler_params=pltpu.CompilerParams(vmem_limit_bytes=SMALL),
        name="relay",
    )(*came)


def owner_kernel(rows, far_flags, *refs):
    came, (own, send) = refs[:SIDE], refs[SIDE:]
    half = CW // 2
    for c, (top, height) in enumerate(chunk_rows(rows, far_flags)):
        blocks = [r.at[pl.ds(top, height)] for r in came]
        total, far = unpack_sum(blocks, rows, far_flags[c])
        own[:, pl.ds(c * half, half)] = total
        if far_flags[c]:
            far = jnp.concatenate([jnp.zeros((LANES - NO // 2, rows), F32), far], axis=0)
            own[:, pl.ds(HALF, LANES)] = far.T
    scale = column_scale(jnp.max(jnp.abs(own[...]), axis=1, keepdims=True))
    send[:, pl.ds(0, HALF)] = encode(own[:, pl.ds(0, HALF)], scale)
    lane = lax.broadcasted_iota(S32, (rows, LANES), 1)
    far = jnp.round(own[:, pl.ds(HALF, LANES)] * (jnp.exp2(scale * (-1.0 / LOG_GRID)) * FULL))
    far = jnp.where(lane == 0, jnp.broadcast_to(scale, (rows, LANES)), far)
    send[:, pl.ds(HALF, LANES)] = far.astype(S32).astype(S16)


def owner(came, rows, far_flags):
    vmem = pl.BlockSpec(memory_space=pltpu.VMEM)
    width = HALF + LANES
    return pl.pallas_call(
        functools.partial(owner_kernel, rows, far_flags),
        out_shape=[pltpu.HBM((rows, width), F32), jax.ShapeDtypeStruct((rows, width), S16)],
        in_specs=[vmem] * SIDE,
        out_specs=[vmem] * 2,
        compiler_params=pltpu.CompilerParams(vmem_limit_bytes=SMALL),
        name="owner",
    )(*came)


def close_kernel(rows, own, came, ranks, energy, pair_sum, spread, out, joined):
    heads = came[:, pl.ds(HALF, LANES)].astype(S32).astype(F32)
    scale = jnp.exp2(heads[:, 0:1] * (1.0 / LOG_GRID)) * (1.0 / FULL)
    plain = came[...].astype(S32).astype(F32) * scale
    slot = lax.broadcasted_iota(S32, (rows, rows), 1)
    back = [(slot == ranks[:, k : k + 1]).astype(F32).astype(BF16) for k in range(2)]
    mine = sort_rows(back[0], own[...])
    other = sort_rows(back[1], plain)
    lane = lax.broadcasted_iota(S32, (rows, LANES), 1)
    off_diagonal = lane < LANES - NO // 2
    edge = HALF - LANES
    joined[:, pl.ds(0, edge)] = mine[:, :edge]
    joined[:, pl.ds(HALF, edge)] = other[:, :edge]
    last_mine, last_other = mine[:, edge:HALF], other[:, edge:HALF]
    joined[:, pl.ds(edge, LANES)] = last_mine + jnp.where(off_diagonal, 0.0, last_other)
    joined[:, pl.ds(HALF + edge, LANES)] = jnp.where(off_diagonal, last_other, mine[:, HALF:] + other[:, HALF:])
    total = None
    for part in halves(joined[...]):
        add = jnp.dot(part, spread[...], preferred_element_type=F32)
        total = add if total is None else total + add
    out[...] = total / (energy[...] - pair_sum[...])


def close(own, came, ranks, energy, pair_sum, spread, rows):
    vmem = pl.BlockSpec(memory_space=pltpu.VMEM)
    return pl.pallas_call(
        functools.partial(close_kernel, rows),
        out_shape=jax.ShapeDtypeStruct((rows, OCC), F32),
        in_specs=[vmem] * 6,
        out_specs=vmem,
        scratch_shapes=[pltpu.VMEM((rows, OCC), F32)],
        compiler_params=pltpu.CompilerParams(vmem_limit_bytes=SMALL),
        name="close",
    )(own, came, ranks, energy, pair_sum, spread)


def trade(pieces, x_core):
    got = [pieces[0]]
    for k in (2, 1, 3):
        perm = []
        for row in range(2 * SIDE):
            for z in range(SIDE):
                for x in range(SIDE):
                    zt, xt = (z, (x + k) % SIDE) if row % 2 == x_core else ((z + k) % SIDE, x)
                    perm.append(((row * SIDE + z) * SIDE + x, (row * SIDE + zt) * SIDE + xt))
        got.append(lax.ppermute(pieces[k], ("row", "col"), perm))
    return got


def shifted_rows(dy, dcore):
    return [(y * 2 + c, (y + dy) % SIDE * 2 + (c + dcore) % 2) for y in range(SIDE) for c in range(2)]


def fetch_along(part):
    return [part] + [lax.ppermute(part, "row", shifted_rows(k, 0)) for k in range(1, SIDE)]


def share(along):
    mine = jnp.stack(along)
    return [mine, lax.ppermute(mine, "row", shifted_rows(0, 1))]


def body(integrals, tile_count, tile_list, amplitudes, pair_energy, occ_energy, partner):
    rows = partner.shape[0]
    groups = SIDE * SIDE
    first, mates_of = pair_orders()
    half = CW // 2
    column_order = np.concatenate(
        [np.concatenate([first[c * half :][:half], mates_of[c * half :][:half]]) for c in range(CHUNKS)]
    )
    pair_ids = jnp.arange(OCC, dtype=S32)
    sort = (pair_ids[:, None] == jnp.asarray(column_order)[None, :]).astype(BF16)
    spread = (jnp.asarray(np.concatenate([first, mates_of]))[:, None] == pair_ids[None, :]).astype(BF16)

    blocks, depth, _ = amplitudes.shape
    sorted_amp = jnp.dot(amplitudes.reshape(blocks * depth, OCC), sort, preferred_element_type=F32).astype(BF16)
    parts = [sorted_amp[:, c * CW : (c + 1) * CW].reshape(blocks, depth, CW) for c in range(CHUNKS)]

    peer = rows // groups
    target = partner // rows % groups
    key_local = partner % rows
    row_ids = jnp.arange(rows, dtype=S32)
    same_target = target[:, None] == target[None, :]
    own_rank = target * peer + jnp.sum(same_target & (row_ids[None, :] < row_ids[:, None]), axis=1)
    mate_rank = target * peer + jnp.sum(same_target & (key_local[None, :] < key_local[:, None]), axis=1)
    both = jnp.concatenate([own_rank, mate_rank]).astype(S32)
    spoken = jnp.broadcast_to(both[None, :], (groups, 2 * rows))
    ranks = lax.all_to_all(spoken, "col", split_axis=0, concat_axis=0, tiled=True)
    along = [fetch_along(part) for part in parts]
    ranks, along[0] = lax.optimization_barrier((ranks, along[0]))
    ranks = jnp.stack([ranks[:, :rows], ranks[:, rows:]])

    row = lax.axis_index("row")
    col = lax.axis_index("col")
    z, x, core = col // SIDE, col % SIDE, row % 2
    place = jnp.stack([row // 2, core, jnp.where(core == 0, x, z), jnp.where(core == 0, z, x)]).astype(S32)
    slots = tile_list[0, 0]
    slot_ids = jnp.arange(slots.shape[0], dtype=S32)
    order = jnp.sum(jnp.where(slots[None, :] == slot_ids[:, None], slot_ids[None, :], 0), axis=1)
    live = (order < tile_count[0, 0]).astype(S32)

    tiles = stage(integrals[0, 0], order, live)
    far_flags = tuple(c == CHUNKS - 1 for c in range(CHUNKS))
    landed = []
    for c in range(CHUNKS):
        sent = product(tiles, share(along[c]), ranks, place, rows, far_flags[c])
        if c > 0:
            sent, landed = lax.optimization_barrier((sent, landed))
        if c + 1 < CHUNKS:
            sent, along[c + 1] = lax.optimization_barrier((sent, along[c + 1]))
        landed += trade(sent, 0)
    own, send = owner(trade(relay(landed, rows, far_flags), 1), rows, far_flags)
    came = lax.all_to_all(send, "col", split_axis=0, concat_axis=0, tiled=True)
    pair_sum = (occ_energy[:, None] + occ_energy[None, :]).reshape(1, OCC)
    back = jnp.stack([own_rank, mate_rank], axis=1).astype(S32)
    return close(own, came, back, pair_energy[:, None], pair_sum, spread, rows)


def solution(mesh):
    return jax.shard_map(
        body,
        mesh=mesh,
        in_specs=(
            P("row", "col", None, None, None),
            P("row", "col"),
            P("row", "col", None),
            P("col", "row", None),
            P(("row", "col")),
            P(),
            P(("row", "col")),
        ),
        out_specs=P(("row", "col"), None),
        check_vma=False,
    )
```

```python
import functools

import numpy as np
import jax
import jax.numpy as jnp
from jax import lax
from jax.experimental import pallas as pl
from jax.experimental.pallas import tpu as pltpu
from jax.sharding import PartitionSpec as P

F32, S32, S16, BF16 = jnp.float32, jnp.int32, jnp.int16, jnp.bfloat16
NO = 32
OCC = NO * NO
HALF = OCC // 2
CHUNKS = 2
CW = OCC // CHUNKS
LANES = 128
SIDE = 4
PAD = 16
LOG_GRID = 200.0
FULL = 32760.0
TINY = 1e-37
VMEM = 20 * 1024 * 1024
SMALL = 16 * 1024 * 1024


def pair_orders():
    first, mates = [], []
    for gap in range(1, NO // 2 + 1):
        for i in range(NO if gap < NO // 2 else NO // 2):
            j = (i + gap) % NO
            first.append(i * NO + j)
            mates.append(j * NO + i)
    at = CW // 2 - NO // 2
    first[at:at] = [i * NO + i for i in range(NO // 2)]
    mates[at:at] = [i * NO + i for i in range(NO // 2, NO)]
    return np.array(first, np.int32), np.array(mates, np.int32)


def column_scale(level):
    return jnp.ceil(jnp.log(jnp.maximum(level, TINY)) * (LOG_GRID / float(np.log(2.0))))


def encode(values, scale):
    return jnp.round(values * (jnp.exp2(scale * (-1.0 / LOG_GRID)) * FULL)).astype(S32).astype(S16)


def decode(coded, scale):
    return coded.astype(S32).astype(F32) * (jnp.exp2(scale * (1.0 / LOG_GRID)) * (1.0 / FULL))


def pack(out_ref, values, far):
    rows, wide = values.shape
    scale = column_scale(jnp.max(jnp.abs(values), axis=0, keepdims=True))
    out_ref[pl.ds(0, rows), :] = encode(values, scale)
    heads = jnp.broadcast_to(scale, (PAD, wide))
    if far is None:
        out_ref[pl.ds(rows, PAD), :] = heads.astype(S32).astype(S16)
        return
    far_scale = column_scale(jnp.max(jnp.abs(far), axis=0, keepdims=True))
    out_ref[pl.ds(rows, PAD), :] = encode(far, far_scale)
    which = lax.broadcasted_iota(S32, (PAD, wide), 0)
    heads = jnp.where(which == 0, heads, jnp.broadcast_to(far_scale, (PAD, wide)))
    out_ref[pl.ds(rows + PAD, PAD), :] = heads.astype(S32).astype(S16)


def unpack_sum(refs, rows, has_far):
    total, far = None, None
    for ref in refs:
        heads = ref[pl.ds(rows + (PAD if has_far else 0), PAD), :].astype(S32).astype(F32)
        part = decode(ref[pl.ds(0, rows), :], heads[0:1])
        total = part if total is None else total + part
        if has_far:
            part = decode(ref[pl.ds(rows, PAD), :], heads[1:2])
            far = part if far is None else far + part
    return total, far


def halves(values):
    high = values.astype(BF16)
    return high, (values - high.astype(F32)).astype(BF16)


def sort_rows(matrix, values):
    high, low = halves(values)
    return jnp.dot(matrix, high, preferred_element_type=F32) + jnp.dot(matrix, low, preferred_element_type=F32)


def product_kernel(has_far, rows, fetch, place_ref, *rest):
    if fetch:
        order_ref, live_ref, tiles_ref, rank_ref = rest[:4]
        amps, outs, v_ref, (first, mates, table, raw, arrived) = rest[4:6], rest[6:10], rest[10], rest[11:]
    else:
        v_ref, rank_ref = rest[:2]
        amps, outs, (first, mates, table, raw) = rest[2:4], rest[4:8], rest[8:]
    tiles, tile, _ = v_ref.shape
    steps = tiles // 4
    half = CW // 2
    groups = SIDE * SIDE
    peer = rows // groups

    def copy(p):
        return pltpu.make_async_copy(tiles_ref.at[order_ref[p]], v_ref.at[p], arrived.at[p])

    def await_tiles(step):
        for j in range(4):

            @pl.when(live_ref[step * 4 + j] > 0)
            def _():
                copy(step * 4 + j).wait()

    if fetch:
        for p in range(tiles):

            @pl.when(live_ref[p] > 0)
            def _():
                copy(p).start()

        def clear(p, carry):
            @pl.when(live_ref[p] <= 0)
            def _():
                v_ref[p] = jnp.zeros((tile, tile), BF16)

            return carry

        lax.fori_loop(0, tiles, clear, 0)

    y, core, here, there = (place_ref[k] for k in range(4))
    depth = amps[0].shape[2]
    for k in range(SIDE):
        chip = lax.rem(y + SIDE - k, SIDE) * 2
        for c in range(2):
            at = (chip + (core if c == 0 else 1 - core)) * depth
            for j in range(4):
                table[pl.ds(pl.multiple_of(j * tile + at, depth), depth), :] = amps[c][k, j]

    def multiply(step, part):
        total = None
        for j in range(4):
            v = v_ref[step * 4 + j]
            t = table[j * tile : (j + 1) * tile, part * half : (part + 1) * half]
            add = jnp.dot(v, t, preferred_element_type=F32)
            total = add if total is None else total + add
        return total

    def sort(step, part, values):
        for b in range(tile // rows):
            block = step * (tile // rows) + b
            rank = rank_ref[part, pl.ds(block, 1), :]
            matrix = (lax.broadcasted_iota(S32, (rows, rows), 0) == rank).astype(F32).astype(BF16)
            done = sort_rows(matrix, values[b * rows : (b + 1) * rows])
            if part == 0:
                first[pl.ds(pl.multiple_of(block * rows, rows), rows), :] = done
            else:
                mates[pl.ds(block, 1)] = done.reshape(1, groups, peer, half)

    def columns(part):
        return pl.ds(part * half, half)

    if fetch:
        await_tiles(0)
    for part in range(2):
        raw[pl.ds(0, tile), columns(part)] = multiply(0, part)

    def turn(step, carry):
        if fetch:
            await_tiles(step)
        before = pl.multiple_of(lax.rem(step + 1, 2) * tile, tile)
        now = pl.multiple_of(lax.rem(step, 2) * tile, tile)
        held = [raw[pl.ds(before, tile), columns(part)] for part in range(2)]
        for part in range(2):
            total = multiply(step, part)
            sort(step - 1, part, held[part])
            raw[pl.ds(now, tile), columns(part)] = total
        return carry

    lax.fori_loop(1, steps, turn, 0)
    for part in range(2):
        sort(steps - 1, part, raw[pl.ds((steps - 1) % 2 * tile, tile), columns(part)])

    for k in range(SIDE):
        for m in range(SIDE):
            near, later = lax.rem(here + k, SIDE), lax.rem(there + m, SIDE)
            owner_id = jnp.where(core == 0, later * SIDE + near, near * SIDE + later)
            base = pl.multiple_of(owner_id * rows, rows)
            mine = first[pl.ds(base, rows), :]
            other = mates[:, pl.ds(owner_id, 1)].reshape(rows, half)
            far = None
            if has_far:
                far = other[:, half - LANES :].T[LANES - NO // 2 :]
                lane = lax.broadcasted_iota(S32, (rows, half), 1)
                other = jnp.where(lane < half - NO // 2, other, 0.0)
            pack(outs[k].at[m], mine + other, far)


def packed_rows(rows, has_far):
    return rows + PAD * (2 if has_far else 1)


def product(tiles, amps, ranks, place, rows, has_far, order=None, live=None):
    count, tile, _ = tiles.shape
    groups = SIDE * SIDE
    half = CW // 2
    fetch = order is not None
    vmem, smem = pl.BlockSpec(memory_space=pltpu.VMEM), pl.BlockSpec(memory_space=pltpu.SMEM)
    out_shape = [jax.ShapeDtypeStruct((SIDE, packed_rows(rows, has_far), half), S16)] * SIDE
    out_specs = [vmem] * SIDE
    scratch = [
        pltpu.VMEM((groups * rows, half), F32),
        pltpu.VMEM((groups, groups, rows // groups, half), F32),
        pltpu.VMEM((4 * tile, CW), BF16),
        pltpu.VMEM((2 * tile, CW), F32),
    ]
    if fetch:
        args = (place, order, live, pltpu.with_memory_space_constraint(tiles, pltpu.HBM), ranks, *amps)
        in_specs = [smem] * 3 + [pl.BlockSpec(memory_space=pl.ANY)] + [vmem] * (1 + len(amps))
        out_shape.append(pltpu.VMEM(tiles.shape, tiles.dtype))
        out_specs.append(vmem)
        scratch.append(pltpu.SemaphoreType.DMA((count,)))
    else:
        args = (place, tiles, ranks, *amps)
        in_specs = [smem] + [vmem] * (2 + len(amps))
    return pl.pallas_call(
        functools.partial(product_kernel, has_far, rows, fetch),
        out_shape=out_shape,
        in_specs=in_specs,
        out_specs=out_specs,
        scratch_shapes=scratch,
        compiler_params=pltpu.CompilerParams(vmem_limit_bytes=VMEM),
        cost_estimate=pl.CostEstimate(
            flops=2 * count * tile * tile * CW, bytes_accessed=4 * tile * CW * 4, transcendentals=0
        ),
        name="product",
    )(*args)


def chunk_rows(rows, far_flags):
    heights = [packed_rows(rows, flag) for flag in far_flags]
    return [(sum(heights[:c]), heights[c]) for c in range(len(heights))]


def relay_kernel(rows, far_flags, *refs):
    ins, outs = refs[:-SIDE], refs[-SIDE:]
    for c, (top, height) in enumerate(chunk_rows(rows, far_flags)):
        for m in range(SIDE):
            blocks = [r.at[m] for r in ins[c * SIDE :][:SIDE]]
            total, far = unpack_sum(blocks, rows, far_flags[c])
            pack(outs[m].at[pl.ds(top, height)], total, far)


def relay(came, rows, far_flags):
    height = sum(h for _, h in chunk_rows(rows, far_flags))
    vmem = pl.BlockSpec(memory_space=pltpu.VMEM)
    return pl.pallas_call(
        functools.partial(relay_kernel, rows, far_flags),
        out_shape=[jax.ShapeDtypeStruct((height, CW // 2), S16)] * SIDE,
        in_specs=[vmem] * len(came),
        out_specs=[vmem] * SIDE,
        compiler_params=pltpu.CompilerParams(vmem_limit_bytes=SMALL),
        name="relay",
    )(*came)


def owner_kernel(rows, far_flags, *refs):
    came, (own, send) = refs[:SIDE], refs[SIDE:]
    half = CW // 2
    for c, (top, height) in enumerate(chunk_rows(rows, far_flags)):
        blocks = [r.at[pl.ds(top, height)] for r in came]
        total, far = unpack_sum(blocks, rows, far_flags[c])
        own[:, pl.ds(c * half, half)] = total
        if far_flags[c]:
            far = jnp.concatenate([jnp.zeros((LANES - NO // 2, rows), F32), far], axis=0)
            own[:, pl.ds(HALF, LANES)] = far.T
    scale = column_scale(jnp.max(jnp.abs(own[...]), axis=1, keepdims=True))
    send[:, pl.ds(0, HALF)] = encode(own[:, pl.ds(0, HALF)], scale)
    lane = lax.broadcasted_iota(S32, (rows, LANES), 1)
    far = jnp.round(own[:, pl.ds(HALF, LANES)] * (jnp.exp2(scale * (-1.0 / LOG_GRID)) * FULL))
    far = jnp.where(lane == 0, jnp.broadcast_to(scale, (rows, LANES)), far)
    send[:, pl.ds(HALF, LANES)] = far.astype(S32).astype(S16)


def owner(came, rows, far_flags):
    vmem = pl.BlockSpec(memory_space=pltpu.VMEM)
    width = HALF + LANES
    return pl.pallas_call(
        functools.partial(owner_kernel, rows, far_flags),
        out_shape=[pltpu.HBM((rows, width), F32), jax.ShapeDtypeStruct((rows, width), S16)],
        in_specs=[vmem] * SIDE,
        out_specs=[vmem] * 2,
        compiler_params=pltpu.CompilerParams(vmem_limit_bytes=SMALL),
        name="owner",
    )(*came)


def close_kernel(rows, own, came, ranks, energy, pair_sum, spread, out, joined):
    heads = came[:, pl.ds(HALF, LANES)].astype(S32).astype(F32)
    scale = jnp.exp2(heads[:, 0:1] * (1.0 / LOG_GRID)) * (1.0 / FULL)
    plain = came[...].astype(S32).astype(F32) * scale
    slot = lax.broadcasted_iota(S32, (rows, rows), 1)
    back = [(slot == ranks[:, k : k + 1]).astype(F32).astype(BF16) for k in range(2)]
    mine = sort_rows(back[0], own[...])
    other = sort_rows(back[1], plain)
    joined[:, pl.ds(0, HALF)] = mine[:, :HALF]
    joined[:, pl.ds(HALF, HALF)] = other[:, :HALF]
    off_diagonal = lax.broadcasted_iota(S32, (rows, LANES), 1) < LANES - NO // 2
    edge = CW // 2 - LANES
    last_mine, last_other = mine[:, edge : edge + LANES], other[:, edge : edge + LANES]
    joined[:, pl.ds(edge, LANES)] = last_mine + jnp.where(off_diagonal, 0.0, last_other)
    joined[:, pl.ds(HALF + edge, LANES)] = jnp.where(off_diagonal, last_other, mine[:, HALF:] + other[:, HALF:])
    total = None
    for part in halves(joined[...]):
        add = jnp.dot(part, spread[...], preferred_element_type=F32)
        total = add if total is None else total + add
    out[...] = total / (energy[...] - pair_sum[...])


def close(own, came, ranks, energy, pair_sum, spread, rows):
    vmem = pl.BlockSpec(memory_space=pltpu.VMEM)
    return pl.pallas_call(
        functools.partial(close_kernel, rows),
        out_shape=jax.ShapeDtypeStruct((rows, OCC), F32),
        in_specs=[vmem] * 6,
        out_specs=vmem,
        scratch_shapes=[pltpu.VMEM((rows, OCC), F32)],
        compiler_params=pltpu.CompilerParams(vmem_limit_bytes=SMALL),
        name="close",
    )(own, came, ranks, energy, pair_sum, spread)


def trade(pieces, x_core):
    got = [pieces[0]]
    for k in (2, 1, 3):
        perm = []
        for row in range(2 * SIDE):
            for z in range(SIDE):
                for x in range(SIDE):
                    zt, xt = (z, (x + k) % SIDE) if row % 2 == x_core else ((z + k) % SIDE, x)
                    perm.append(((row * SIDE + z) * SIDE + x, (row * SIDE + zt) * SIDE + xt))
        got.append(lax.ppermute(pieces[k], ("row", "col"), perm))
    return got


def shifted_rows(dy, dcore):
    return [(y * 2 + c, (y + dy) % SIDE * 2 + (c + dcore) % 2) for y in range(SIDE) for c in range(2)]


def fetch_along(part):
    return [part] + [lax.ppermute(part, "row", shifted_rows(k, 0)) for k in range(1, SIDE)]


def share(along):
    mine = jnp.stack(along)
    return [mine, lax.ppermute(mine, "row", shifted_rows(0, 1))]


def body(integrals, tile_count, tile_list, amplitudes, pair_energy, occ_energy, partner):
    rows = partner.shape[0]
    groups = SIDE * SIDE
    first, mates_of = pair_orders()
    half = CW // 2
    column_order = np.concatenate(
        [np.concatenate([first[c * half :][:half], mates_of[c * half :][:half]]) for c in range(CHUNKS)]
    )
    pair_ids = jnp.arange(OCC, dtype=S32)
    sort = (pair_ids[:, None] == jnp.asarray(column_order)[None, :]).astype(BF16)
    spread = (jnp.asarray(np.concatenate([first, mates_of]))[:, None] == pair_ids[None, :]).astype(BF16)

    blocks, depth, _ = amplitudes.shape
    sorted_amp = jnp.dot(amplitudes.reshape(blocks * depth, OCC), sort, preferred_element_type=F32).astype(BF16)
    parts = [sorted_amp[:, c * CW : (c + 1) * CW].reshape(blocks, depth, CW) for c in range(CHUNKS)]

    peer = rows // groups
    target = partner // rows % groups
    key_local = partner % rows
    row_ids = jnp.arange(rows, dtype=S32)
    same_target = target[:, None] == target[None, :]
    own_rank = target * peer + jnp.sum(same_target & (row_ids[None, :] < row_ids[:, None]), axis=1)
    mate_rank = target * peer + jnp.sum(same_target & (key_local[None, :] < key_local[:, None]), axis=1)
    both = jnp.concatenate([own_rank, mate_rank]).astype(S32)
    spoken = jnp.broadcast_to(both[None, :], (groups, 2 * rows))
    ranks = lax.all_to_all(spoken, "col", split_axis=0, concat_axis=0, tiled=True)
    along = [fetch_along(part) for part in parts]
    ranks, along[0] = lax.optimization_barrier((ranks, along[0]))
    ranks = jnp.stack([ranks[:, :rows], ranks[:, rows:]])

    row = lax.axis_index("row")
    col = lax.axis_index("col")
    z, x, core = col // SIDE, col % SIDE, row % 2
    place = jnp.stack([row // 2, core, jnp.where(core == 0, x, z), jnp.where(core == 0, z, x)]).astype(S32)
    slots = tile_list[0, 0]
    slot_ids = jnp.arange(slots.shape[0], dtype=S32)
    order = jnp.sum(jnp.where(slots[None, :] == slot_ids[:, None], slot_ids[None, :], 0), axis=1)
    live = (order < tile_count[0, 0]).astype(S32)

    tiles = integrals[0, 0]
    far_flags = tuple(c == 0 for c in range(CHUNKS))
    landed = []
    for c in range(CHUNKS):
        if c == 0:
            *sent, tiles = product(tiles, share(along[c]), ranks, place, rows, far_flags[c], order, live)
        else:
            sent = product(tiles, share(along[c]), ranks, place, rows, far_flags[c])
        if c > 0:
            sent, landed = lax.optimization_barrier((sent, landed))
        if c + 1 < CHUNKS:
            sent, along[c + 1] = lax.optimization_barrier((sent, along[c + 1]))
        landed += trade(sent, 0)
    own, send = owner(trade(relay(landed, rows, far_flags), 1), rows, far_flags)
    own = pltpu.with_memory_space_constraint(own, pltpu.HBM)
    came = lax.all_to_all(send, "col", split_axis=0, concat_axis=0, tiled=True)
    pair_sum = (occ_energy[:, None] + occ_energy[None, :]).reshape(1, OCC)
    back = jnp.stack([own_rank, mate_rank], axis=1).astype(S32)
    return close(own, came, back, pair_energy[:, None], pair_sum, spread, rows)


def solution(mesh):
    return jax.shard_map(
        body,
        mesh=mesh,
        in_specs=(
            P("row", "col", None, None, None),
            P("row", "col"),
            P("row", "col", None),
            P("col", "row", None),
            P(("row", "col")),
            P(),
            P(("row", "col")),
        ),
        out_specs=P(("row", "col"), None),
        check_vma=False,
    )
```

```python
import functools

import numpy as np
import jax
import jax.numpy as jnp
from jax import lax
from jax.experimental import pallas as pl
from jax.experimental.pallas import tpu as pltpu
from jax.sharding import PartitionSpec as P

F32, S32, S16, BF16 = jnp.float32, jnp.int32, jnp.int16, jnp.bfloat16
NO = 32
OCC = NO * NO
HALF = OCC // 2
CHUNKS = 2
CW = OCC // CHUNKS
LANES = 128
SIDE = 4
PAD = 16
LOG_GRID = 200.0
FULL = 32760.0
TINY = 1e-37
VMEM = 16 * 1024 * 1024
SMALL = 16 * 1024 * 1024


def pair_orders():
    first, mates = [], []
    for gap in range(1, NO // 2 + 1):
        for i in range(NO if gap < NO // 2 else NO // 2):
            j = (i + gap) % NO
            first.append(i * NO + j)
            mates.append(j * NO + i)
    at = CW // 2 - NO // 2
    first[at:at] = [i * NO + i for i in range(NO // 2)]
    mates[at:at] = [i * NO + i for i in range(NO // 2, NO)]
    return np.array(first, np.int32), np.array(mates, np.int32)


def column_scale(level):
    return jnp.ceil(jnp.log(jnp.maximum(level, TINY)) * (LOG_GRID / float(np.log(2.0))))


def encode(values, scale):
    return jnp.round(values * (jnp.exp2(scale * (-1.0 / LOG_GRID)) * FULL)).astype(S32).astype(S16)


def decode(coded, scale):
    return coded.astype(S32).astype(F32) * (jnp.exp2(scale * (1.0 / LOG_GRID)) * (1.0 / FULL))


def pack(out_ref, values, far):
    rows, wide = values.shape
    scale = column_scale(jnp.max(jnp.abs(values), axis=0, keepdims=True))
    out_ref[pl.ds(0, rows), :] = encode(values, scale)
    heads = jnp.broadcast_to(scale, (PAD, wide))
    if far is None:
        out_ref[pl.ds(rows, PAD), :] = heads.astype(S32).astype(S16)
        return
    far_scale = column_scale(jnp.max(jnp.abs(far), axis=0, keepdims=True))
    out_ref[pl.ds(rows, PAD), :] = encode(far, far_scale)
    which = lax.broadcasted_iota(S32, (PAD, wide), 0)
    heads = jnp.where(which == 0, heads, jnp.broadcast_to(far_scale, (PAD, wide)))
    out_ref[pl.ds(rows + PAD, PAD), :] = heads.astype(S32).astype(S16)


def unpack_sum(refs, rows, has_far):
    total, far = None, None
    for ref in refs:
        heads = ref[pl.ds(rows + (PAD if has_far else 0), PAD), :].astype(S32).astype(F32)
        part = decode(ref[pl.ds(0, rows), :], heads[0:1])
        total = part if total is None else total + part
        if has_far:
            part = decode(ref[pl.ds(rows, PAD), :], heads[1:2])
            far = part if far is None else far + part
    return total, far


def halves(values):
    high = values.astype(BF16)
    return high, (values - high.astype(F32)).astype(BF16)


def sort_rows(matrix, values):
    high, low = halves(values)
    return jnp.dot(matrix, high, preferred_element_type=F32) + jnp.dot(matrix, low, preferred_element_type=F32)


def product_kernel(has_far, rows, fetch, place_ref, *rest):
    if fetch:
        order_ref, live_ref, tiles_ref, rank_ref = rest[:4]
        amps, outs, v_ref, (first, mates, table, raw, arrived) = rest[4:6], rest[6:10], rest[10], rest[11:]
    else:
        v_ref, rank_ref = rest[:2]
        amps, outs, (first, mates, table, raw) = rest[2:4], rest[4:8], rest[8:]
    tiles, tile, _ = v_ref.shape
    steps = tiles // 4
    half = CW // 2
    groups = SIDE * SIDE
    peer = rows // groups

    def copy(p):
        return pltpu.make_async_copy(tiles_ref.at[order_ref[p]], v_ref.at[p], arrived.at[p])

    def request_tiles(step):
        for j in range(4):

            @pl.when(live_ref[step * 4 + j] > 0)
            def _():
                copy(step * 4 + j).start()

    def await_tiles(step):
        for j in range(4):

            @pl.when(live_ref[step * 4 + j] > 0)
            def _():
                copy(step * 4 + j).wait()

    if fetch:
        request_tiles(0)

        def clear(p, carry):
            @pl.when(live_ref[p] <= 0)
            def _():
                v_ref[p] = jnp.zeros((tile, tile), BF16)

            return carry

        lax.fori_loop(0, tiles, clear, 0)

    y, core, here, there = (place_ref[k] for k in range(4))
    depth = amps[0].shape[2]
    for k in range(SIDE):
        chip = lax.rem(y + SIDE - k, SIDE) * 2
        for c in range(2):
            at = (chip + (core if c == 0 else 1 - core)) * depth
            for j in range(4):
                table[pl.ds(pl.multiple_of(j * tile + at, depth), depth), :] = amps[c][k, j]

    def multiply(step, part):
        total = None
        for j in range(4):
            v = v_ref[step * 4 + j]
            t = table[j * tile : (j + 1) * tile, part * half : (part + 1) * half]
            add = jnp.dot(v, t, preferred_element_type=F32)
            total = add if total is None else total + add
        return total

    def sort(step, part, values):
        for b in range(tile // rows):
            block = step * (tile // rows) + b
            rank = rank_ref[part, pl.ds(block, 1), :]
            matrix = (lax.broadcasted_iota(S32, (rows, rows), 0) == rank).astype(F32).astype(BF16)
            done = sort_rows(matrix, values[b * rows : (b + 1) * rows])
            if part == 0:
                first[pl.ds(pl.multiple_of(block * rows, rows), rows), :] = done
            else:
                mates[pl.ds(block, 1)] = done.reshape(1, groups, peer, half)

    def columns(part):
        return pl.ds(part * half, half)

    if fetch:
        request_tiles(1)
        await_tiles(0)
    for part in range(2):
        raw[pl.ds(0, tile), columns(part)] = multiply(0, part)

    def turn(step, carry):
        if fetch:

            @pl.when(step + 1 < steps)
            def _():
                request_tiles(step + 1)

            await_tiles(step)
        before = pl.multiple_of(lax.rem(step + 1, 2) * tile, tile)
        now = pl.multiple_of(lax.rem(step, 2) * tile, tile)
        held = [raw[pl.ds(before, tile), columns(part)] for part in range(2)]
        for part in range(2):
            total = multiply(step, part)
            sort(step - 1, part, held[part])
            raw[pl.ds(now, tile), columns(part)] = total
        return carry

    lax.fori_loop(1, steps, turn, 0)
    for part in range(2):
        sort(steps - 1, part, raw[pl.ds((steps - 1) % 2 * tile, tile), columns(part)])

    for k in range(SIDE):
        for m in range(SIDE):
            near, later = lax.rem(here + k, SIDE), lax.rem(there + m, SIDE)
            owner_id = jnp.where(core == 0, later * SIDE + near, near * SIDE + later)
            base = pl.multiple_of(owner_id * rows, rows)
            mine = first[pl.ds(base, rows), :]
            other = mates[:, pl.ds(owner_id, 1)].reshape(rows, half)
            far = None
            if has_far:
                far = other[:, half - LANES :].T[LANES - NO // 2 :]
                lane = lax.broadcasted_iota(S32, (rows, half), 1)
                other = jnp.where(lane < half - NO // 2, other, 0.0)
            pack(outs[k].at[m], mine + other, far)


def packed_rows(rows, has_far):
    return rows + PAD * (2 if has_far else 1)


def product(tiles, amps, ranks, place, rows, has_far, order=None, live=None):
    count, tile, _ = tiles.shape
    groups = SIDE * SIDE
    half = CW // 2
    fetch = order is not None
    vmem, smem = pl.BlockSpec(memory_space=pltpu.VMEM), pl.BlockSpec(memory_space=pltpu.SMEM)
    out_shape = [jax.ShapeDtypeStruct((SIDE, packed_rows(rows, has_far), half), S16)] * SIDE
    out_specs = [vmem] * SIDE
    scratch = [
        pltpu.VMEM((groups * rows, half), F32),
        pltpu.VMEM((groups, groups, rows // groups, half), F32),
        pltpu.VMEM((4 * tile, CW), BF16),
        pltpu.VMEM((2 * tile, CW), F32),
    ]
    if fetch:
        args = (place, order, live, pltpu.with_memory_space_constraint(tiles, pltpu.HBM), ranks, *amps)
        in_specs = [smem] * 3 + [pl.BlockSpec(memory_space=pl.ANY)] + [vmem] * (1 + len(amps))
        out_shape.append(pltpu.VMEM(tiles.shape, tiles.dtype))
        out_specs.append(vmem)
        scratch.append(pltpu.SemaphoreType.DMA((count,)))
    else:
        args = (place, tiles, ranks, *amps)
        in_specs = [smem] + [vmem] * (2 + len(amps))
    return pl.pallas_call(
        functools.partial(product_kernel, has_far, rows, fetch),
        out_shape=out_shape,
        in_specs=in_specs,
        out_specs=out_specs,
        scratch_shapes=scratch,
        compiler_params=pltpu.CompilerParams(vmem_limit_bytes=VMEM),
        cost_estimate=pl.CostEstimate(
            flops=2 * count * tile * tile * CW, bytes_accessed=4 * tile * CW * 4, transcendentals=0
        ),
        name="product",
    )(*args)


def chunk_rows(rows, far_flags):
    heights = [packed_rows(rows, flag) for flag in far_flags]
    return [(sum(heights[:c]), heights[c]) for c in range(len(heights))]


def relay_kernel(rows, far_flags, *refs):
    ins, outs = refs[:-SIDE], refs[-SIDE:]
    for c, (top, height) in enumerate(chunk_rows(rows, far_flags)):
        for m in range(SIDE):
            blocks = [r.at[m] for r in ins[c * SIDE :][:SIDE]]
            total, far = unpack_sum(blocks, rows, far_flags[c])
            pack(outs[m].at[pl.ds(top, height)], total, far)


def relay(came, rows, far_flags):
    height = sum(h for _, h in chunk_rows(rows, far_flags))
    vmem = pl.BlockSpec(memory_space=pltpu.VMEM)
    return pl.pallas_call(
        functools.partial(relay_kernel, rows, far_flags),
        out_shape=[jax.ShapeDtypeStruct((height, CW // 2), S16)] * SIDE,
        in_specs=[vmem] * len(came),
        out_specs=[vmem] * SIDE,
        compiler_params=pltpu.CompilerParams(vmem_limit_bytes=SMALL),
        name="relay",
    )(*came)


def owner_kernel(rows, far_flags, *refs):
    came, (own, send) = refs[:SIDE], refs[SIDE:]
    half = CW // 2
    for c, (top, height) in enumerate(chunk_rows(rows, far_flags)):
        blocks = [r.at[pl.ds(top, height)] for r in came]
        total, far = unpack_sum(blocks, rows, far_flags[c])
        own[:, pl.ds(c * half, half)] = total
        if far_flags[c]:
            far = jnp.concatenate([jnp.zeros((LANES - NO // 2, rows), F32), far], axis=0)
            own[:, pl.ds(HALF, LANES)] = far.T
    scale = column_scale(jnp.max(jnp.abs(own[...]), axis=1, keepdims=True))
    send[:, pl.ds(0, HALF)] = encode(own[:, pl.ds(0, HALF)], scale)
    lane = lax.broadcasted_iota(S32, (rows, LANES), 1)
    far = jnp.round(own[:, pl.ds(HALF, LANES)] * (jnp.exp2(scale * (-1.0 / LOG_GRID)) * FULL))
    far = jnp.where(lane == 0, jnp.broadcast_to(scale, (rows, LANES)), far)
    send[:, pl.ds(HALF, LANES)] = far.astype(S32).astype(S16)


def owner(came, rows, far_flags):
    vmem = pl.BlockSpec(memory_space=pltpu.VMEM)
    width = HALF + LANES
    return pl.pallas_call(
        functools.partial(owner_kernel, rows, far_flags),
        out_shape=[pltpu.HBM((rows, width), F32), jax.ShapeDtypeStruct((rows, width), S16)],
        in_specs=[vmem] * SIDE,
        out_specs=[vmem] * 2,
        compiler_params=pltpu.CompilerParams(vmem_limit_bytes=SMALL),
        name="owner",
    )(*came)


def back_to_place(ranks, values):
    rows = values.shape[0]
    matrix = (lax.broadcasted_iota(S32, (rows, rows), 1) == ranks).astype(F32).astype(BF16)
    return sort_rows(matrix, values)


def place_columns(values, spread):
    high, low = halves(values)
    return jnp.dot(high, spread, preferred_element_type=F32) + jnp.dot(low, spread, preferred_element_type=F32)


def mine_kernel(own, ranks, spread, out):
    mine = back_to_place(ranks[:, 0:1], own[...])
    at = HALF + CW // 2 - LANES
    out[...] = place_columns(mine[:, :HALF], spread[pl.ds(0, HALF), :]) + place_columns(
        mine[:, HALF:], spread[pl.ds(at, LANES), :]
    )


def close_kernel(mine, came, ranks, energy, pair_sum, spread, out):
    heads = came[:, pl.ds(HALF, LANES)].astype(S32).astype(F32)
    scale = jnp.exp2(heads[:, 0:1] * (1.0 / LOG_GRID)) * (1.0 / FULL)
    other = back_to_place(ranks[:, 1:2], came[...].astype(S32).astype(F32) * scale)
    edge = CW // 2 - LANES
    last = other[:, edge : edge + LANES]
    off_diagonal = lax.broadcasted_iota(S32, last.shape, 1) < LANES - NO // 2
    mates = jnp.concatenate(
        [other[:, :edge], jnp.where(off_diagonal, last, other[:, HALF:]), other[:, edge + LANES : HALF]], axis=1
    )
    total = place_columns(mates, spread[pl.ds(HALF, HALF), :])
    total = total + place_columns(jnp.where(off_diagonal, 0.0, last), spread[pl.ds(edge, LANES), :])
    out[...] = (mine[...] + total) / (energy[...] - pair_sum[...])


def last_call(kernel, name, args, result):
    vmem = pl.BlockSpec(memory_space=pltpu.VMEM)
    return pl.pallas_call(
        kernel,
        out_shape=result,
        in_specs=[vmem] * len(args),
        out_specs=vmem,
        compiler_params=pltpu.CompilerParams(vmem_limit_bytes=SMALL),
        cost_estimate=pl.CostEstimate(flops=4 * OCC**3 // 4, bytes_accessed=2 * OCC * OCC, transcendentals=0),
        name=name,
    )(*args)


def trade(pieces, x_core):
    got = [pieces[0]]
    for k in (2, 1, 3):
        perm = []
        for row in range(2 * SIDE):
            for z in range(SIDE):
                for x in range(SIDE):
                    zt, xt = (z, (x + k) % SIDE) if row % 2 == x_core else ((z + k) % SIDE, x)
                    perm.append(((row * SIDE + z) * SIDE + x, (row * SIDE + zt) * SIDE + xt))
        got.append(lax.ppermute(pieces[k], ("row", "col"), perm))
    return got


def shifted_rows(dy, dcore):
    return [(y * 2 + c, (y + dy) % SIDE * 2 + (c + dcore) % 2) for y in range(SIDE) for c in range(2)]


def fetch_along(part):
    far, next_to, last = (lax.ppermute(part, "row", shifted_rows(k, 0)) for k in (2, 1, 3))
    return [part, next_to, far, last]


def share(along):
    mine = jnp.stack(along)
    return [mine, lax.ppermute(mine, "row", shifted_rows(0, 1))]


def body(integrals, tile_count, tile_list, amplitudes, pair_energy, occ_energy, partner):
    rows = partner.shape[0]
    groups = SIDE * SIDE
    first, mates_of = pair_orders()
    half = CW // 2
    column_order = np.concatenate(
        [np.concatenate([first[c * half :][:half], mates_of[c * half :][:half]]) for c in range(CHUNKS)]
    )
    pair_ids = jnp.arange(OCC, dtype=S32)
    sort = (pair_ids[:, None] == jnp.asarray(column_order)[None, :]).astype(BF16)
    spread = (jnp.asarray(np.concatenate([first, mates_of]))[:, None] == pair_ids[None, :]).astype(BF16)

    blocks, depth, _ = amplitudes.shape
    sorted_amp = jnp.dot(amplitudes.reshape(blocks * depth, OCC), sort, preferred_element_type=F32).astype(BF16)
    parts = [sorted_amp[:, c * CW : (c + 1) * CW].reshape(blocks, depth, CW) for c in range(CHUNKS)]

    peer = rows // groups
    target = partner // rows % groups
    key_local = partner % rows
    row_ids = jnp.arange(rows, dtype=S32)
    same_target = target[:, None] == target[None, :]
    own_rank = target * peer + jnp.sum(same_target & (row_ids[None, :] < row_ids[:, None]), axis=1)
    mate_rank = target * peer + jnp.sum(same_target & (key_local[None, :] < key_local[:, None]), axis=1)
    both = jnp.concatenate([own_rank, mate_rank]).astype(S32)
    spoken = jnp.broadcast_to(both[None, :], (groups, 2 * rows))
    ranks = lax.all_to_all(spoken, "col", split_axis=0, concat_axis=0, tiled=True)
    along = [fetch_along(part) for part in parts]
    ranks, along[0] = lax.optimization_barrier((ranks, along[0]))
    ranks = jnp.stack([ranks[:, :rows], ranks[:, rows:]])

    row = lax.axis_index("row")
    col = lax.axis_index("col")
    z, x, core = col // SIDE, col % SIDE, row % 2
    place = jnp.stack([row // 2, core, jnp.where(core == 0, x, z), jnp.where(core == 0, z, x)]).astype(S32)
    slots = tile_list[0, 0]
    slot_ids = jnp.arange(slots.shape[0], dtype=S32)
    order = jnp.sum(jnp.where(slots[None, :] == slot_ids[:, None], slot_ids[None, :], 0), axis=1)
    live = (order < tile_count[0, 0]).astype(S32)

    tiles = integrals[0, 0]
    far_flags = tuple(c == 0 for c in range(CHUNKS))
    landed = []
    for c in range(CHUNKS):
        if c == 0:
            *sent, tiles = product(tiles, share(along[c]), ranks, place, rows, far_flags[c], order, live)
        else:
            sent = product(tiles, share(along[c]), ranks, place, rows, far_flags[c])
        if c > 0:
            sent, landed = lax.optimization_barrier((sent, landed))
        if c + 1 < CHUNKS:
            sent, along[c + 1] = lax.optimization_barrier((sent, along[c + 1]))
        landed += trade(sent, 0)
    own, send = owner(trade(relay(landed, rows, far_flags), 1), rows, far_flags)
    came = lax.all_to_all(send, "col", split_axis=0, concat_axis=0, tiled=True)
    pair_sum = (occ_energy[:, None] + occ_energy[None, :]).reshape(1, OCC)
    back = jnp.stack([own_rank, mate_rank], axis=1).astype(S32)
    own = pltpu.with_memory_space_constraint(own, pltpu.HBM)
    mine = last_call(mine_kernel, "mine", (own, back, spread), pltpu.HBM((rows, OCC), F32))
    mine = pltpu.with_memory_space_constraint(mine, pltpu.HBM)
    args = (mine, came, back, pair_energy[:, None], pair_sum, spread)
    return last_call(close_kernel, "close", args, jax.ShapeDtypeStruct((rows, OCC), F32))


def solution(mesh):
    return jax.shard_map(
        body,
        mesh=mesh,
        in_specs=(
            P("row", "col", None, None, None),
            P("row", "col"),
            P("row", "col", None),
            P("col", "row", None),
            P(("row", "col")),
            P(),
            P(("row", "col")),
        ),
        out_specs=P(("row", "col"), None),
        check_vma=False,
    )
```

```python
import functools

import numpy as np
import jax
import jax.numpy as jnp
from jax import lax
from jax.experimental import pallas as pl
from jax.experimental.pallas import tpu as pltpu
from jax.sharding import PartitionSpec as P

F32, S32, S16, BF16 = jnp.float32, jnp.int32, jnp.int16, jnp.bfloat16
NO = 32
OCC = NO * NO
HALF = OCC // 2
CHUNKS = 2
CW = OCC // CHUNKS
LANES = 128
SIDE = 4
PAD = 16
LOG_GRID = 200.0
FULL = 32760.0
TINY = 1e-37
VMEM = 16 * 1024 * 1024
SMALL = 16 * 1024 * 1024


def pair_orders():
    first, mates = [], []
    for gap in range(1, NO // 2 + 1):
        for i in range(NO if gap < NO // 2 else NO // 2):
            j = (i + gap) % NO
            first.append(i * NO + j)
            mates.append(j * NO + i)
    at = CW // 2 - NO // 2
    first[at:at] = [i * NO + i for i in range(NO // 2)]
    mates[at:at] = [i * NO + i for i in range(NO // 2, NO)]
    return np.array(first, np.int32), np.array(mates, np.int32)


def column_scale(level):
    return jnp.ceil(jnp.log(jnp.maximum(level, TINY)) * (LOG_GRID / float(np.log(2.0))))


def encode(values, scale):
    return jnp.round(values * (jnp.exp2(scale * (-1.0 / LOG_GRID)) * FULL)).astype(S32).astype(S16)


def decode(coded, scale):
    return coded.astype(S32).astype(F32) * (jnp.exp2(scale * (1.0 / LOG_GRID)) * (1.0 / FULL))


def pack(out_ref, values, far):
    rows, wide = values.shape
    scale = column_scale(jnp.max(jnp.abs(values), axis=0, keepdims=True))
    out_ref[pl.ds(0, rows), :] = encode(values, scale)
    heads = jnp.broadcast_to(scale, (PAD, wide))
    if far is None:
        out_ref[pl.ds(rows, PAD), :] = heads.astype(S32).astype(S16)
        return
    far_scale = column_scale(jnp.max(jnp.abs(far), axis=0, keepdims=True))
    out_ref[pl.ds(rows, PAD), :] = encode(far, far_scale)
    which = lax.broadcasted_iota(S32, (PAD, wide), 0)
    heads = jnp.where(which == 0, heads, jnp.broadcast_to(far_scale, (PAD, wide)))
    out_ref[pl.ds(rows + PAD, PAD), :] = heads.astype(S32).astype(S16)


def unpack_sum(refs, rows, has_far):
    total, far = None, None
    for ref in refs:
        heads = ref[pl.ds(rows + (PAD if has_far else 0), PAD), :].astype(S32).astype(F32)
        part = decode(ref[pl.ds(0, rows), :], heads[0:1])
        total = part if total is None else total + part
        if has_far:
            part = decode(ref[pl.ds(rows, PAD), :], heads[1:2])
            far = part if far is None else far + part
    return total, far


def halves(values):
    high = values.astype(BF16)
    return high, (values - high.astype(F32)).astype(BF16)


def sort_rows(matrix, values):
    high, low = halves(values)
    return jnp.dot(matrix, high, preferred_element_type=F32) + jnp.dot(matrix, low, preferred_element_type=F32)


def product_kernel(has_far, rows, fetch, place_ref, *rest):
    if fetch:
        order_ref, live_ref, tiles_ref, rank_ref = rest[:4]
        amps, outs, v_ref, (first, mates, table, raw, arrived) = rest[4:6], rest[6:10], rest[10], rest[11:]
    else:
        v_ref, rank_ref = rest[:2]
        amps, outs, (first, mates, table, raw) = rest[2:4], rest[4:8], rest[8:]
    tiles, tile, _ = v_ref.shape
    steps = tiles // 4
    half = CW // 2
    groups = SIDE * SIDE
    peer = rows // groups

    def copy(p):
        return pltpu.make_async_copy(tiles_ref.at[order_ref[p]], v_ref.at[p], arrived.at[p])

    def request_tiles(step):
        for j in range(4):

            @pl.when(live_ref[step * 4 + j] > 0)
            def _():
                copy(step * 4 + j).start()

    def await_tiles(step):
        for j in range(4):

            @pl.when(live_ref[step * 4 + j] > 0)
            def _():
                copy(step * 4 + j).wait()

    if fetch:
        request_tiles(0)

        def clear(p, carry):
            @pl.when(live_ref[p] <= 0)
            def _():
                v_ref[p] = jnp.zeros((tile, tile), BF16)

            return carry

        lax.fori_loop(0, tiles, clear, 0)

    y, core, here, there = (place_ref[k] for k in range(4))
    depth = amps[0].shape[2]
    for k in range(SIDE):
        chip = lax.rem(y + SIDE - k, SIDE) * 2
        for c in range(2):
            at = (chip + (core if c == 0 else 1 - core)) * depth
            for j in range(4):
                table[pl.ds(pl.multiple_of(j * tile + at, depth), depth), :] = amps[c][k, j]

    def multiply(step, part):
        total = None
        for j in range(4):
            v = v_ref[step * 4 + j]
            t = table[j * tile : (j + 1) * tile, part * half : (part + 1) * half]
            add = jnp.dot(v, t, preferred_element_type=F32)
            total = add if total is None else total + add
        return total

    def sort(step, part, values):
        for b in range(tile // rows):
            block = step * (tile // rows) + b
            rank = rank_ref[part, pl.ds(block, 1), :]
            matrix = (lax.broadcasted_iota(S32, (rows, rows), 0) == rank).astype(F32).astype(BF16)
            done = sort_rows(matrix, values[b * rows : (b + 1) * rows])
            if part == 0:
                first[pl.ds(pl.multiple_of(block * rows, rows), rows), :] = done
            else:
                mates[pl.ds(block, 1)] = done.reshape(1, groups, peer, half)

    def columns(part):
        return pl.ds(part * half, half)

    if fetch:
        request_tiles(1)
        await_tiles(0)
    for part in range(2):
        raw[pl.ds(0, tile), columns(part)] = multiply(0, part)

    def turn(step, carry):
        if fetch:

            @pl.when(step + 1 < steps)
            def _():
                request_tiles(step + 1)

            await_tiles(step)
        before = pl.multiple_of(lax.rem(step + 1, 2) * tile, tile)
        now = pl.multiple_of(lax.rem(step, 2) * tile, tile)
        held = [raw[pl.ds(before, tile), columns(part)] for part in range(2)]
        for part in range(2):
            total = multiply(step, part)
            sort(step - 1, part, held[part])
            raw[pl.ds(now, tile), columns(part)] = total
        return carry

    lax.fori_loop(1, steps, turn, 0)
    for part in range(2):
        sort(steps - 1, part, raw[pl.ds((steps - 1) % 2 * tile, tile), columns(part)])

    for k in range(SIDE):
        for m in range(SIDE):
            near, later = lax.rem(here + k, SIDE), lax.rem(there + m, SIDE)
            owner_id = jnp.where(core == 0, later * SIDE + near, near * SIDE + later)
            base = pl.multiple_of(owner_id * rows, rows)
            mine = first[pl.ds(base, rows), :]
            other = mates[:, pl.ds(owner_id, 1)].reshape(rows, half)
            far = None
            if has_far:
                far = other[:, half - LANES :].T[LANES - NO // 2 :]
                lane = lax.broadcasted_iota(S32, (rows, half), 1)
                other = jnp.where(lane < half - NO // 2, other, 0.0)
            pack(outs[k].at[m], mine + other, far)


def packed_rows(rows, has_far):
    return rows + PAD * (2 if has_far else 1)


def product(tiles, amps, ranks, place, rows, has_far, order=None, live=None):
    count, tile, _ = tiles.shape
    groups = SIDE * SIDE
    half = CW // 2
    fetch = order is not None
    vmem, smem = pl.BlockSpec(memory_space=pltpu.VMEM), pl.BlockSpec(memory_space=pltpu.SMEM)
    out_shape = [jax.ShapeDtypeStruct((SIDE, packed_rows(rows, has_far), half), S16)] * SIDE
    out_specs = [vmem] * SIDE
    scratch = [
        pltpu.VMEM((groups * rows, half), F32),
        pltpu.VMEM((groups, groups, rows // groups, half), F32),
        pltpu.VMEM((4 * tile, CW), BF16),
        pltpu.VMEM((2 * tile, CW), F32),
    ]
    if fetch:
        args = (place, order, live, pltpu.with_memory_space_constraint(tiles, pltpu.HBM), ranks, *amps)
        in_specs = [smem] * 3 + [pl.BlockSpec(memory_space=pl.ANY)] + [vmem] * (1 + len(amps))
        out_shape.append(pltpu.VMEM(tiles.shape, tiles.dtype))
        out_specs.append(vmem)
        scratch.append(pltpu.SemaphoreType.DMA((count,)))
    else:
        args = (place, tiles, ranks, *amps)
        in_specs = [smem] + [vmem] * (2 + len(amps))
    return pl.pallas_call(
        functools.partial(product_kernel, has_far, rows, fetch),
        out_shape=out_shape,
        in_specs=in_specs,
        out_specs=out_specs,
        scratch_shapes=scratch,
        compiler_params=pltpu.CompilerParams(vmem_limit_bytes=VMEM),
        cost_estimate=pl.CostEstimate(
            flops=2 * count * tile * tile * CW, bytes_accessed=4 * tile * CW * 4, transcendentals=0
        ),
        name="product",
    )(*args)


def chunk_rows(rows, far_flags):
    heights = [packed_rows(rows, flag) for flag in far_flags]
    return [(sum(heights[:c]), heights[c]) for c in range(len(heights))]


def relay_kernel(rows, far_flags, *refs):
    ins, outs = refs[:-SIDE], refs[-SIDE:]
    for c, (top, height) in enumerate(chunk_rows(rows, far_flags)):
        for m in range(SIDE):
            blocks = [r.at[m] for r in ins[c * SIDE :][:SIDE]]
            total, far = unpack_sum(blocks, rows, far_flags[c])
            pack(outs[m].at[pl.ds(top, height)], total, far)


def relay(came, rows, far_flags):
    height = sum(h for _, h in chunk_rows(rows, far_flags))
    vmem = pl.BlockSpec(memory_space=pltpu.VMEM)
    return pl.pallas_call(
        functools.partial(relay_kernel, rows, far_flags),
        out_shape=[jax.ShapeDtypeStruct((height, CW // 2), S16)] * SIDE,
        in_specs=[vmem] * len(came),
        out_specs=[vmem] * SIDE,
        compiler_params=pltpu.CompilerParams(vmem_limit_bytes=SMALL),
        name="relay",
    )(*came)


def owner_kernel(rows, far_flags, *refs):
    came, (own, send) = refs[:SIDE], refs[SIDE:]
    half = CW // 2
    for c, (top, height) in enumerate(chunk_rows(rows, far_flags)):
        blocks = [r.at[pl.ds(top, height)] for r in came]
        total, far = unpack_sum(blocks, rows, far_flags[c])
        own[:, pl.ds(c * half, half)] = total
        if far_flags[c]:
            far = jnp.concatenate([jnp.zeros((LANES - NO // 2, rows), F32), far], axis=0)
            own[:, pl.ds(HALF, LANES)] = far.T
    scale = column_scale(jnp.max(jnp.abs(own[...]), axis=1, keepdims=True))
    send[:, pl.ds(0, HALF)] = encode(own[:, pl.ds(0, HALF)], scale)
    lane = lax.broadcasted_iota(S32, (rows, LANES), 1)
    far = jnp.round(own[:, pl.ds(HALF, LANES)] * (jnp.exp2(scale * (-1.0 / LOG_GRID)) * FULL))
    far = jnp.where(lane == 0, jnp.broadcast_to(scale, (rows, LANES)), far)
    send[:, pl.ds(HALF, LANES)] = far.astype(S32).astype(S16)


def owner(came, rows, far_flags):
    vmem = pl.BlockSpec(memory_space=pltpu.VMEM)
    width = HALF + LANES
    return pl.pallas_call(
        functools.partial(owner_kernel, rows, far_flags),
        out_shape=[pltpu.HBM((rows, width), F32), jax.ShapeDtypeStruct((rows, width), S16)],
        in_specs=[vmem] * SIDE,
        out_specs=[vmem] * 2,
        compiler_params=pltpu.CompilerParams(vmem_limit_bytes=SMALL),
        name="owner",
    )(*came)


def back_to_place(ranks, values):
    rows = values.shape[0]
    matrix = (lax.broadcasted_iota(S32, (rows, rows), 1) == ranks).astype(F32).astype(BF16)
    return sort_rows(matrix, values)


def place_columns(values, spread):
    high, low = halves(values)
    return jnp.dot(high, spread, preferred_element_type=F32) + jnp.dot(low, spread, preferred_element_type=F32)


def mine_kernel(own, ranks, spread, out):
    mine = back_to_place(ranks[:, 0:1], own[...])
    at = HALF + CW // 2 - LANES
    out[...] = place_columns(mine[:, :HALF], spread[pl.ds(0, HALF), :]) + place_columns(
        mine[:, HALF:], spread[pl.ds(at, LANES), :]
    )


def close_kernel(mine, came, ranks, energy, pair_sum, spread, out):
    heads = came[:, pl.ds(HALF, LANES)].astype(S32).astype(F32)
    scale = jnp.exp2(heads[:, 0:1] * (1.0 / LOG_GRID)) * (1.0 / FULL)
    other = back_to_place(ranks[:, 1:2], came[...].astype(S32).astype(F32) * scale)
    edge = CW // 2 - LANES
    last = other[:, edge : edge + LANES]
    off_diagonal = lax.broadcasted_iota(S32, last.shape, 1) < LANES - NO // 2
    mates = jnp.concatenate(
        [other[:, :edge], jnp.where(off_diagonal, last, other[:, HALF:]), other[:, edge + LANES : HALF]], axis=1
    )
    total = place_columns(mates, spread[pl.ds(HALF, HALF), :])
    total = total + place_columns(jnp.where(off_diagonal, 0.0, last), spread[pl.ds(edge, LANES), :])
    out[...] = (mine[...] + total) / (energy[...] - pair_sum[...])


def last_call(kernel, name, args, result):
    vmem = pl.BlockSpec(memory_space=pltpu.VMEM)
    return pl.pallas_call(
        kernel,
        out_shape=result,
        in_specs=[vmem] * len(args),
        out_specs=vmem,
        compiler_params=pltpu.CompilerParams(vmem_limit_bytes=SMALL),
        cost_estimate=pl.CostEstimate(flops=4 * OCC**3 // 4, bytes_accessed=2 * OCC * OCC, transcendentals=0),
        name=name,
    )(*args)


def trade(pieces, x_core):
    got = [pieces[0]]
    for k in (2, 1, 3):
        perm = []
        for row in range(2 * SIDE):
            for z in range(SIDE):
                for x in range(SIDE):
                    zt, xt = (z, (x + k) % SIDE) if row % 2 == x_core else ((z + k) % SIDE, x)
                    perm.append(((row * SIDE + z) * SIDE + x, (row * SIDE + zt) * SIDE + xt))
        got.append(lax.ppermute(pieces[k], ("row", "col"), perm))
    return got


def shifted_rows(dy, dcore):
    return [(y * 2 + c, (y + dy) % SIDE * 2 + (c + dcore) % 2) for y in range(SIDE) for c in range(2)]


def fetch_along(part):
    far, next_to, last = (lax.ppermute(part, "row", shifted_rows(k, 0)) for k in (2, 1, 3))
    return [part, next_to, far, last]


def share(along):
    mine = jnp.stack(along)
    return [mine, lax.ppermute(mine, "row", shifted_rows(0, 1))]


def body(integrals, tile_count, tile_list, amplitudes, pair_energy, occ_energy, partner):
    rows = partner.shape[0]
    groups = SIDE * SIDE
    first, mates_of = pair_orders()
    half = CW // 2
    column_order = np.concatenate(
        [np.concatenate([first[c * half :][:half], mates_of[c * half :][:half]]) for c in range(CHUNKS)]
    )
    pair_ids = jnp.arange(OCC, dtype=S32)
    sort = (pair_ids[:, None] == jnp.asarray(column_order)[None, :]).astype(BF16)
    spread = (jnp.asarray(np.concatenate([first, mates_of]))[:, None] == pair_ids[None, :]).astype(BF16)

    blocks, depth, _ = amplitudes.shape
    sorted_amp = jnp.dot(amplitudes.reshape(blocks * depth, OCC), sort, preferred_element_type=F32).astype(BF16)
    parts = [sorted_amp[:, c * CW : (c + 1) * CW].reshape(blocks, depth, CW) for c in range(CHUNKS)]

    peer = rows // groups
    target = partner // rows % groups
    key_local = partner % rows
    row_ids = jnp.arange(rows, dtype=S32)
    same_target = target[:, None] == target[None, :]
    own_rank = target * peer + jnp.sum(same_target & (row_ids[None, :] < row_ids[:, None]), axis=1)
    mate_rank = target * peer + jnp.sum(same_target & (key_local[None, :] < key_local[:, None]), axis=1)
    both = jnp.concatenate([own_rank, mate_rank]).astype(S32)
    spoken = jnp.broadcast_to(both[None, :], (groups, 2 * rows))
    ranks = lax.all_to_all(spoken, "col", split_axis=0, concat_axis=0, tiled=True)
    along = [fetch_along(part) for part in parts]
    ranks = jnp.stack([ranks[:, :rows], ranks[:, rows:]])
    row, col = lax.axis_index("row"), lax.axis_index("col")
    z, x, core = col // SIDE, col % SIDE, row % 2
    place = jnp.stack([row // 2, core, jnp.where(core == 0, x, z), jnp.where(core == 0, z, x)]).astype(S32)
    slots = tile_list[0, 0]
    slot_ids = jnp.arange(slots.shape[0], dtype=S32)
    order = jnp.sum(jnp.where(slots[None, :] == slot_ids[:, None], slot_ids[None, :], 0), axis=1)
    live = (order < tile_count[0, 0]).astype(S32)
    ranks, order, live, place, along[0] = lax.optimization_barrier((ranks, order, live, place, along[0]))

    tiles = integrals[0, 0]
    far_flags = tuple(c == 0 for c in range(CHUNKS))
    landed = []
    for c in range(CHUNKS):
        if c == 0:
            *sent, tiles = product(tiles, share(along[c]), ranks, place, rows, far_flags[c], order, live)
        else:
            sent = product(tiles, share(along[c]), ranks, place, rows, far_flags[c])
        if c > 0:
            sent, landed = lax.optimization_barrier((sent, landed))
        if c + 1 < CHUNKS:
            sent, along[c + 1] = lax.optimization_barrier((sent, along[c + 1]))
        landed += trade(sent, 0)
    own, send = owner(trade(relay(landed, rows, far_flags), 1), rows, far_flags)
    came = lax.all_to_all(send, "col", split_axis=0, concat_axis=0, tiled=True)
    pair_sum = (occ_energy[:, None] + occ_energy[None, :]).reshape(1, OCC)
    back = jnp.stack([own_rank, mate_rank], axis=1).astype(S32)
    own = pltpu.with_memory_space_constraint(own, pltpu.HBM)
    mine = last_call(mine_kernel, "mine", (own, back, spread), pltpu.HBM((rows, OCC), F32))
    mine = pltpu.with_memory_space_constraint(mine, pltpu.HBM)
    args = (mine, came, back, pair_energy[:, None], pair_sum, spread)
    return last_call(close_kernel, "close", args, jax.ShapeDtypeStruct((rows, OCC), F32))


def solution(mesh):
    return jax.shard_map(
        body,
        mesh=mesh,
        in_specs=(
            P("row", "col", None, None, None),
            P("row", "col"),
            P("row", "col", None),
            P("col", "row", None),
            P(("row", "col")),
            P(),
            P(("row", "col")),
        ),
        out_specs=P(("row", "col"), None),
        check_vma=False,
    )
```

```python
import functools

import numpy as np
import jax
import jax.numpy as jnp
from jax import lax
from jax.experimental import pallas as pl
from jax.experimental.pallas import tpu as pltpu
from jax.sharding import PartitionSpec as P

F32, S32, S16, BF16 = jnp.float32, jnp.int32, jnp.int16, jnp.bfloat16
NO = 32
OCC = NO * NO
HALF = OCC // 2
CHUNKS = 2
CW = OCC // CHUNKS
LANES = 128
SIDE = 4
PAD = 16
LOG_GRID = 200.0
FULL = 32760.0
TINY = 1e-37
VMEM = 16 * 1024 * 1024
SMALL = 16 * 1024 * 1024


def pair_orders():
    first, mates = [], []
    for gap in range(1, NO // 2 + 1):
        for i in range(NO if gap < NO // 2 else NO // 2):
            j = (i + gap) % NO
            first.append(i * NO + j)
            mates.append(j * NO + i)
    at = CW // 2 - NO // 2
    first[at:at] = [i * NO + i for i in range(NO // 2)]
    mates[at:at] = [i * NO + i for i in range(NO // 2, NO)]
    return np.array(first, np.int32), np.array(mates, np.int32)


def column_scale(level):
    return jnp.ceil(jnp.log(jnp.maximum(level, TINY)) * (LOG_GRID / float(np.log(2.0))))


def encode(values, scale):
    return jnp.round(values * (jnp.exp2(scale * (-1.0 / LOG_GRID)) * FULL)).astype(S32).astype(S16)


def decode(coded, scale):
    return coded.astype(S32).astype(F32) * (jnp.exp2(scale * (1.0 / LOG_GRID)) * (1.0 / FULL))


def pack(out_ref, values, far):
    rows, wide = values.shape
    scale = column_scale(jnp.max(jnp.abs(values), axis=0, keepdims=True))
    out_ref[pl.ds(0, rows), :] = encode(values, scale)
    heads = jnp.broadcast_to(scale, (PAD, wide))
    if far is None:
        out_ref[pl.ds(rows, PAD), :] = heads.astype(S32).astype(S16)
        return
    far_scale = column_scale(jnp.max(jnp.abs(far), axis=0, keepdims=True))
    out_ref[pl.ds(rows, PAD), :] = encode(far, far_scale)
    which = lax.broadcasted_iota(S32, (PAD, wide), 0)
    heads = jnp.where(which == 0, heads, jnp.broadcast_to(far_scale, (PAD, wide)))
    out_ref[pl.ds(rows + PAD, PAD), :] = heads.astype(S32).astype(S16)


def unpack_sum(refs, rows, has_far):
    total, far = None, None
    for ref in refs:
        heads = ref[pl.ds(rows + (PAD if has_far else 0), PAD), :].astype(S32).astype(F32)
        part = decode(ref[pl.ds(0, rows), :], heads[0:1])
        total = part if total is None else total + part
        if has_far:
            part = decode(ref[pl.ds(rows, PAD), :], heads[1:2])
            far = part if far is None else far + part
    return total, far


def halves(values):
    high = values.astype(BF16)
    return high, (values - high.astype(F32)).astype(BF16)


def sort_rows(matrix, values):
    high, low = halves(values)
    return jnp.dot(matrix, high, preferred_element_type=F32) + jnp.dot(matrix, low, preferred_element_type=F32)


def product_kernel(has_far, rows, fetch, place_ref, *rest):
    if fetch:
        order_ref, live_ref, tiles_ref, rank_ref = rest[:4]
        amps, outs, v_ref, (first, mates, table, raw, arrived) = rest[4:6], rest[6:10], rest[10], rest[11:]
    else:
        v_ref, rank_ref = rest[:2]
        amps, outs, (first, mates, table, raw) = rest[2:4], rest[4:8], rest[8:]
    tiles, tile, _ = v_ref.shape
    steps = tiles // 4
    half = CW // 2
    groups = SIDE * SIDE
    peer = rows // groups

    def copy(p):
        return pltpu.make_async_copy(tiles_ref.at[order_ref[p]], v_ref.at[p], arrived.at[p])

    def request_tiles(step):
        for j in range(4):

            @pl.when(live_ref[step * 4 + j] > 0)
            def _():
                copy(step * 4 + j).start()

    def await_tiles(step):
        for j in range(4):

            @pl.when(live_ref[step * 4 + j] > 0)
            def _():
                copy(step * 4 + j).wait()

    if fetch:
        request_tiles(0)

        def clear(p, carry):
            @pl.when(live_ref[p] <= 0)
            def _():
                v_ref[p] = jnp.zeros((tile, tile), BF16)

            return carry

        lax.fori_loop(0, tiles, clear, 0)

    y, core, here, there = (place_ref[k] for k in range(4))
    depth = amps[0].shape[2]
    for k in range(SIDE):
        chip = lax.rem(y + SIDE - k, SIDE) * 2
        for c in range(2):
            at = (chip + (core if c == 0 else 1 - core)) * depth
            for j in range(4):
                table[pl.ds(pl.multiple_of(j * tile + at, depth), depth), :] = amps[c][k, j]

    def multiply(step, part):
        total = None
        for j in range(4):
            v = v_ref[step * 4 + j]
            t = table[j * tile : (j + 1) * tile, part * half : (part + 1) * half]
            add = jnp.dot(v, t, preferred_element_type=F32)
            total = add if total is None else total + add
        return total

    def sort(step, part, values):
        for b in range(tile // rows):
            block = step * (tile // rows) + b
            rank = rank_ref[part, pl.ds(block, 1), :]
            matrix = (lax.broadcasted_iota(S32, (rows, rows), 0) == rank).astype(F32).astype(BF16)
            done = sort_rows(matrix, values[b * rows : (b + 1) * rows])
            if part == 0:
                first[pl.ds(pl.multiple_of(block * rows, rows), rows), :] = done
            else:
                mates[pl.ds(block, 1)] = done.reshape(1, groups, peer, half)

    def columns(part):
        return pl.ds(part * half, half)

    if fetch:
        request_tiles(1)
        await_tiles(0)
    for part in range(2):
        raw[pl.ds(0, tile), columns(part)] = multiply(0, part)

    def turn(step, carry):
        if fetch:

            @pl.when(step + 1 < steps)
            def _():
                request_tiles(step + 1)

            await_tiles(step)
        before = pl.multiple_of(lax.rem(step + 1, 2) * tile, tile)
        now = pl.multiple_of(lax.rem(step, 2) * tile, tile)
        held = [raw[pl.ds(before, tile), columns(part)] for part in range(2)]
        for part in range(2):
            total = multiply(step, part)
            sort(step - 1, part, held[part])
            raw[pl.ds(now, tile), columns(part)] = total
        return carry

    lax.fori_loop(1, steps, turn, 0)
    for part in range(2):
        sort(steps - 1, part, raw[pl.ds((steps - 1) % 2 * tile, tile), columns(part)])

    for k in range(SIDE):
        for m in range(SIDE):
            near, later = lax.rem(here + k, SIDE), lax.rem(there + m, SIDE)
            owner_id = jnp.where(core == 0, later * SIDE + near, near * SIDE + later)
            base = pl.multiple_of(owner_id * rows, rows)
            mine = first[pl.ds(base, rows), :]
            other = mates[:, pl.ds(owner_id, 1)].reshape(rows, half)
            far = None
            if has_far:
                far = other[:, half - LANES :].T[LANES - NO // 2 :]
                lane = lax.broadcasted_iota(S32, (rows, half), 1)
                other = jnp.where(lane < half - NO // 2, other, 0.0)
            pack(outs[k].at[m], mine + other, far)


def packed_rows(rows, has_far):
    return rows + PAD * (2 if has_far else 1)


def product(tiles, amps, ranks, place, rows, has_far, order=None, live=None):
    count, tile, _ = tiles.shape
    groups = SIDE * SIDE
    half = CW // 2
    fetch = order is not None
    vmem, smem = pl.BlockSpec(memory_space=pltpu.VMEM), pl.BlockSpec(memory_space=pltpu.SMEM)
    out_shape = [jax.ShapeDtypeStruct((SIDE, packed_rows(rows, has_far), half), S16)] * SIDE
    out_specs = [vmem] * SIDE
    scratch = [
        pltpu.VMEM((groups * rows, half), F32),
        pltpu.VMEM((groups, groups, rows // groups, half), F32),
        pltpu.VMEM((4 * tile, CW), BF16),
        pltpu.VMEM((2 * tile, CW), F32),
    ]
    if fetch:
        args = (place, order, live, pltpu.with_memory_space_constraint(tiles, pltpu.HBM), ranks, *amps)
        in_specs = [smem] * 3 + [pl.BlockSpec(memory_space=pl.ANY)] + [vmem] * (1 + len(amps))
        out_shape.append(pltpu.VMEM(tiles.shape, tiles.dtype))
        out_specs.append(vmem)
        scratch.append(pltpu.SemaphoreType.DMA((count,)))
    else:
        args = (place, tiles, ranks, *amps)
        in_specs = [smem] + [vmem] * (2 + len(amps))
    return pl.pallas_call(
        functools.partial(product_kernel, has_far, rows, fetch),
        out_shape=out_shape,
        in_specs=in_specs,
        out_specs=out_specs,
        scratch_shapes=scratch,
        compiler_params=pltpu.CompilerParams(vmem_limit_bytes=VMEM),
        cost_estimate=pl.CostEstimate(
            flops=2 * count * tile * tile * CW, bytes_accessed=4 * tile * CW * 4, transcendentals=0
        ),
        name="product",
    )(*args)


def chunk_rows(rows, far_flags):
    heights = [packed_rows(rows, flag) for flag in far_flags]
    return [(sum(heights[:c]), heights[c]) for c in range(len(heights))]


def relay_kernel(rows, far_flags, *refs):
    ins, outs = refs[:-SIDE], refs[-SIDE:]
    for c, (top, height) in enumerate(chunk_rows(rows, far_flags)):
        for m in range(SIDE):
            blocks = [r.at[m] for r in ins[c * SIDE :][:SIDE]]
            total, far = unpack_sum(blocks, rows, far_flags[c])
            pack(outs[m].at[pl.ds(top, height)], total, far)


def relay(came, rows, far_flags):
    height = sum(h for _, h in chunk_rows(rows, far_flags))
    vmem = pl.BlockSpec(memory_space=pltpu.VMEM)
    return pl.pallas_call(
        functools.partial(relay_kernel, rows, far_flags),
        out_shape=[jax.ShapeDtypeStruct((height, CW // 2), S16)] * SIDE,
        in_specs=[vmem] * len(came),
        out_specs=[vmem] * SIDE,
        compiler_params=pltpu.CompilerParams(vmem_limit_bytes=SMALL),
        name="relay",
    )(*came)


def owner_kernel(rows, far_flags, *refs):
    came, (own, send) = refs[:SIDE], refs[SIDE:]
    half = CW // 2
    for c, (top, height) in enumerate(chunk_rows(rows, far_flags)):
        blocks = [r.at[pl.ds(top, height)] for r in came]
        total, far = unpack_sum(blocks, rows, far_flags[c])
        own[:, pl.ds(c * half, half)] = total
        if far_flags[c]:
            far = jnp.concatenate([jnp.zeros((LANES - NO // 2, rows), F32), far], axis=0)
            own[:, pl.ds(HALF, LANES)] = far.T
    scale = column_scale(jnp.max(jnp.abs(own[...]), axis=1, keepdims=True))
    send[:, pl.ds(0, HALF)] = encode(own[:, pl.ds(0, HALF)], scale)
    lane = lax.broadcasted_iota(S32, (rows, LANES), 1)
    far = jnp.round(own[:, pl.ds(HALF, LANES)] * (jnp.exp2(scale * (-1.0 / LOG_GRID)) * FULL))
    far = jnp.where(lane == 0, jnp.broadcast_to(scale, (rows, LANES)), far)
    send[:, pl.ds(HALF, LANES)] = far.astype(S32).astype(S16)


def owner(came, rows, far_flags):
    vmem = pl.BlockSpec(memory_space=pltpu.VMEM)
    width = HALF + LANES
    return pl.pallas_call(
        functools.partial(owner_kernel, rows, far_flags),
        out_shape=[pltpu.HBM((rows, width), F32), jax.ShapeDtypeStruct((rows, width), S16)],
        in_specs=[vmem] * SIDE,
        out_specs=[vmem] * 2,
        compiler_params=pltpu.CompilerParams(vmem_limit_bytes=SMALL),
        name="owner",
    )(*came)


def back_to_place(ranks, values):
    rows = values.shape[0]
    matrix = (lax.broadcasted_iota(S32, (rows, rows), 1) == ranks).astype(F32).astype(BF16)
    return sort_rows(matrix, values)


def place_columns(values, spread):
    high, low = halves(values)
    return jnp.dot(high, spread, preferred_element_type=F32) + jnp.dot(low, spread, preferred_element_type=F32)


def mine_kernel(own, ranks, spread, out):
    mine = back_to_place(ranks[:, 0:1], own[...])
    at = HALF + CW // 2 - LANES
    out[...] = place_columns(mine[:, :HALF], spread[pl.ds(0, HALF), :]) + place_columns(
        mine[:, HALF:], spread[pl.ds(at, LANES), :]
    )


def close_kernel(mine, came, ranks, energy, pair_sum, spread, out):
    heads = came[:, pl.ds(HALF, LANES)].astype(S32).astype(F32)
    scale = jnp.exp2(heads[:, 0:1] * (1.0 / LOG_GRID)) * (1.0 / FULL)
    other = back_to_place(ranks[:, 1:2], came[...].astype(S32).astype(F32) * scale)
    edge = CW // 2 - LANES
    last = other[:, edge : edge + LANES]
    off_diagonal = lax.broadcasted_iota(S32, last.shape, 1) < LANES - NO // 2
    mates = jnp.concatenate(
        [other[:, :edge], jnp.where(off_diagonal, last, other[:, HALF:]), other[:, edge + LANES : HALF]], axis=1
    )
    total = place_columns(mates, spread[pl.ds(HALF, HALF), :])
    total = total + place_columns(jnp.where(off_diagonal, 0.0, last), spread[pl.ds(edge, LANES), :])
    out[...] = (mine[...] + total) / (energy[...] - pair_sum[...])


def last_call(kernel, name, args, result):
    vmem = pl.BlockSpec(memory_space=pltpu.VMEM)
    return pl.pallas_call(
        kernel,
        out_shape=result,
        in_specs=[vmem] * len(args),
        out_specs=vmem,
        compiler_params=pltpu.CompilerParams(vmem_limit_bytes=SMALL),
        cost_estimate=pl.CostEstimate(flops=4 * OCC**3 // 4, bytes_accessed=2 * OCC * OCC, transcendentals=0),
        name=name,
    )(*args)


def trade(pieces, x_core):
    got = [pieces[0]]
    for k in (2, 1, 3):
        perm = []
        for row in range(2 * SIDE):
            for z in range(SIDE):
                for x in range(SIDE):
                    zt, xt = (z, (x + k) % SIDE) if row % 2 == x_core else ((z + k) % SIDE, x)
                    perm.append(((row * SIDE + z) * SIDE + x, (row * SIDE + zt) * SIDE + xt))
        got.append(lax.ppermute(pieces[k], ("row", "col"), perm))
    return got


def shifted_rows(dy, dcore):
    return [(y * 2 + c, (y + dy) % SIDE * 2 + (c + dcore) % 2) for y in range(SIDE) for c in range(2)]


def fetch_along(part):
    far, next_to, last = (lax.ppermute(part, "row", shifted_rows(k, 0)) for k in (2, 1, 3))
    return [part, next_to, far, last]


def share(along):
    mine = jnp.stack(along)
    return [mine, lax.ppermute(mine, "row", shifted_rows(0, 1))]


def body(integrals, tile_count, tile_list, amplitudes, pair_energy, occ_energy, partner):
    rows = partner.shape[0]
    groups = SIDE * SIDE
    first, mates_of = pair_orders()
    half = CW // 2
    column_order = np.concatenate(
        [np.concatenate([first[c * half :][:half], mates_of[c * half :][:half]]) for c in range(CHUNKS)]
    )
    pair_ids = jnp.arange(OCC, dtype=S32)
    sort = (pair_ids[:, None] == jnp.asarray(column_order)[None, :]).astype(BF16)
    spread = (jnp.asarray(np.concatenate([first, mates_of]))[:, None] == pair_ids[None, :]).astype(BF16)

    blocks, depth, _ = amplitudes.shape
    flat_amps = amplitudes.reshape(blocks * depth, OCC)
    parts = []
    for c in range(CHUNKS):
        part = jnp.dot(flat_amps, sort[:, c * CW : (c + 1) * CW], preferred_element_type=F32)
        parts.append(part.astype(BF16).reshape(blocks, depth, CW))

    peer = rows // groups
    target = partner // rows % groups
    key_local = partner % rows
    row_ids = jnp.arange(rows, dtype=S32)
    same_target = target[:, None] == target[None, :]
    own_rank = target * peer + jnp.sum(same_target & (row_ids[None, :] < row_ids[:, None]), axis=1)
    mate_rank = target * peer + jnp.sum(same_target & (key_local[None, :] < key_local[:, None]), axis=1)
    both = jnp.concatenate([own_rank, mate_rank]).astype(S32)
    spoken = jnp.broadcast_to(both[None, :], (groups, 2 * rows))
    ranks = lax.all_to_all(spoken, "col", split_axis=0, concat_axis=0, tiled=True)
    along = [fetch_along(parts[0])]
    ranks = jnp.stack([ranks[:, :rows], ranks[:, rows:]])
    row, col = lax.axis_index("row"), lax.axis_index("col")
    z, x, core = col // SIDE, col % SIDE, row % 2
    place = jnp.stack([row // 2, core, jnp.where(core == 0, x, z), jnp.where(core == 0, z, x)]).astype(S32)
    slots = tile_list[0, 0]
    slot_ids = jnp.arange(slots.shape[0], dtype=S32)
    order = jnp.sum(jnp.where(slots[None, :] == slot_ids[:, None], slot_ids[None, :], 0), axis=1)
    live = (order < tile_count[0, 0]).astype(S32)
    ready = (ranks, order, live, place, parts, along)
    ranks, order, live, place, parts, along = lax.optimization_barrier(ready)
    along += [fetch_along(part) for part in parts[1:]]

    tiles = integrals[0, 0]
    far_flags = tuple(c == 0 for c in range(CHUNKS))
    landed = []
    for c in range(CHUNKS):
        if c == 0:
            *sent, tiles = product(tiles, share(along[c]), ranks, place, rows, far_flags[c], order, live)
        else:
            sent = product(tiles, share(along[c]), ranks, place, rows, far_flags[c])
        if c > 0:
            sent, landed = lax.optimization_barrier((sent, landed))
        if c + 1 < CHUNKS:
            sent, along[c + 1] = lax.optimization_barrier((sent, along[c + 1]))
        landed += trade(sent, 0)
    own, send = owner(trade(relay(landed, rows, far_flags), 1), rows, far_flags)
    came = lax.all_to_all(send, "col", split_axis=0, concat_axis=0, tiled=True)
    pair_sum = (occ_energy[:, None] + occ_energy[None, :]).reshape(1, OCC)
    back = jnp.stack([own_rank, mate_rank], axis=1).astype(S32)
    own = pltpu.with_memory_space_constraint(own, pltpu.HBM)
    mine = last_call(mine_kernel, "mine", (own, back, spread), pltpu.HBM((rows, OCC), F32))
    mine = pltpu.with_memory_space_constraint(mine, pltpu.HBM)
    args = (mine, came, back, pair_energy[:, None], pair_sum, spread)
    return last_call(close_kernel, "close", args, jax.ShapeDtypeStruct((rows, OCC), F32))


def solution(mesh):
    return jax.shard_map(
        body,
        mesh=mesh,
        in_specs=(
            P("row", "col", None, None, None),
            P("row", "col"),
            P("row", "col", None),
            P("col", "row", None),
            P(("row", "col")),
            P(),
            P(("row", "col")),
        ),
        out_specs=P(("row", "col"), None),
        check_vma=False,
    )
```
